32 devices in a mesh: row: 4 (over z), col: 8 (over y, x, core).
Axes of the slice: x: 2, y: 2, z: 4, core: 2. Of those that a mesh axis runs over, the one named last changes fastest.
Arguments:
- blocks: bfloat16 [2048, 128, 128], P(('row', 'col'))
- owners: int32 [2048], P(('row', 'col')), may hold values from 0 to 7, as said below
- places: int32 [2048], P(('row', 'col')), may hold values from 0 to 127, as said below
- panel_matrix: bfloat16 [64, 128, 512], P('col', 'row'), may hold values from -6 to 6
Outputs:
- inflated: float32 [8192, 512], P(('row', 'col'))
The draws below stay inside these ranges and needn't reach their ends.
Inputs may be any that keep to these rules, and one draw needn't show every extreme that they name: `owners`: on each device at most 16 slots name the same owner; for each index of row one owner is named by exactly 16 slots of every device with that row index. `places`: two slots on devices of the same row index that name the same owner never have the same place.
All inputs are finite; a program needn't handle non-finite values.
Results may differ from the reference program's by a relative error of at most 0.0003.
Values may be sent and summed in bfloat16 or wider, within the bound.
A program may use at most 128 MiB of HBM per device.

```python
import math
import jax
import jax.numpy as jnp
from jax import lax

BS = 128
CB = 8
PW = 512
NB = 64
RB = 16
S_DEV = 64
CAP = 16
N_ROW = 4
N_COL = 8


def slot_layout(key):
    devices = N_ROW * N_COL
    buckets = N_COL * CAP
    grid_cells = RB * CB
    key_score = jax.random.fold_in(key, 101)
    key_level = jax.random.fold_in(key, 202)
    key_filled = jax.random.fold_in(key, 303)
    key_shuffle = jax.random.fold_in(key, 404)
    key_place = jax.random.fold_in(key, 505)
    row_of = jnp.arange(devices, dtype=jnp.int32) // N_COL
    col_of = jnp.arange(devices, dtype=jnp.int32) % N_COL
    bucket_owner = jnp.arange(buckets, dtype=jnp.int32) // CAP
    priority = jax.random.randint(key_level, (N_ROW, N_COL), 0, 4)
    filled = jax.random.randint(key_filled, (N_ROW,), 0, N_COL)
    random_part = jax.random.randint(key_score, (devices, buckets), 0, 1 << 20)
    levels = priority[row_of][:, bucket_owner]
    scores = (random_part + levels * (1 << 18)) * buckets + jnp.arange(buckets, dtype=jnp.int32)[None, :]
    chosen_full = bucket_owner[None, :] == filled[row_of][:, None]
    scores = scores + jnp.where(chosen_full, 1 << 30, 0)
    chosen = lax.top_k(scores, S_DEV)[1].astype(jnp.int32)
    shuffle_keys = jax.random.randint(key_shuffle, (devices, S_DEV), 0, 1 << 20) * S_DEV + jnp.arange(S_DEV, dtype=jnp.int32)[None, :]
    shuffle = jnp.argsort(shuffle_keys, axis=1)
    chosen = jnp.take_along_axis(chosen, shuffle, axis=1)
    owners = chosen // CAP
    bucket_rank = chosen % CAP
    place_keys = jax.random.randint(key_place, (N_ROW, N_COL, grid_cells), 0, 1 << 20) * grid_cells + jnp.arange(grid_cells, dtype=jnp.int32)
    orders = jnp.argsort(place_keys, axis=2).astype(jnp.int32)
    position = col_of[:, None] * CAP + bucket_rank
    places = orders[row_of[:, None], owners, position]
    return (owners.reshape(-1).astype(jnp.int32), places.reshape(-1).astype(jnp.int32))


def draw_owners(key, part):
    return slot_layout(key)[0]


def draw_places(key, part):
    return slot_layout(key)[1]


def draw_blocks(key, part):
    total_slots = N_ROW * N_COL * S_DEV
    base_scale = (BS * N_COL * S_DEV / RB) ** (-0.5)
    growth = (jnp.arange(total_slots, dtype=jnp.int32) // (S_DEV * N_COL)).astype(jnp.float32) / max(N_ROW - 1, 1)
    values = jax.random.normal(key, (total_slots, BS, BS), jnp.float32) * jnp.sqrt(1.0 + 2.0 * growth)[:, None, None]
    return (values * base_scale).astype(jnp.bfloat16)


def block_scale(rng, dims, shards, least, high):
    def one(dim, shards_of):
        draws = jax.random.uniform(jax.random.fold_in(jax.random.fold_in(rng, 6), dim), (shards_of,), jnp.float32, least / len(shards), high / len(shards))
        return jnp.repeat(jnp.exp(draws), dims[dim] // shards_of).reshape((-1,) + (1,) * (len(dims) - dim - 1))

    gain = one(*shards[0])
    for cut in shards[1:]:
        gain = gain * one(*cut)
    return gain


def noise(stream_key, extent, deviation, limit, cuts=(), held_as=jnp.bfloat16):
    drawn = jax.random.normal(stream_key, extent, jnp.float32) * deviation
    if len(cuts) > 0:
        drawn = block_scale(stream_key, extent, cuts, -0.22, 0.18) * drawn
    return jnp.clip(drawn, min=-limit, max=limit).astype(held_as)


def setup_inputs(seed: int = 0) -> dict:
    arg_keys = jax.random.split(jax.random.key(seed), 5)
    return {
        "blocks": draw_blocks(jax.random.fold_in(arg_keys[4], 71), 0),
        "owners": draw_owners(jax.random.fold_in(arg_keys[4], 71), 0),
        "places": draw_places(jax.random.fold_in(arg_keys[4], 71), 0),
        "panel_matrix": noise(arg_keys[3], (NB, BS, PW), 1.0, 6.0, ((0, 8), (1, 4))),
    }


epsilon = 1e-6


def reference(blocks, owners, places, panel_matrix):
    total_slots = blocks.shape[0]
    slot_ids = jnp.arange(total_slots, dtype=jnp.int32)
    block_row = (slot_ids // (S_DEV * N_COL)) * RB + places // CB
    block_col = owners * CB + places % CB
    group_size = math.gcd(total_slots, 512)
    turn_count = total_slots // group_size

    def add_group(partial_value, turn_index):
        offset = turn_index * group_size
        tiles = lax.dynamic_slice_in_dim(blocks, offset, group_size, 0).astype(jnp.float32)
        rows_here = lax.dynamic_slice_in_dim(block_row, offset, group_size, 0)
        cols_here = lax.dynamic_slice_in_dim(block_col, offset, group_size, 0)
        pieces = panel_matrix[cols_here].astype(jnp.float32)
        product = jnp.einsum("sab,sbp->sap", tiles, pieces)
        return partial_value.at[rows_here].add(product), None

    start_sum = jnp.zeros((NB, BS, PW), jnp.float32)
    expanded = lax.scan(add_group, start_sum, jnp.arange(turn_count, dtype=jnp.int32))[0]
    squares = expanded * expanded
    col_mean = jnp.sum(squares, axis=(0, 1)) / (NB * BS)
    return (squares / (col_mean + epsilon)).reshape(NB * BS, PW)
```

```python
import functools

import jax
import jax.numpy as jnp
from jax import lax
from jax.experimental import pallas as pl
from jax.experimental.pallas import tpu as pltpu
from jax.sharding import PartitionSpec as P

epsilon = 1e-06
CHIPS = 4
PARTS = 2
UNROLL = 8
MESH = pl.DeviceIdType.MESH


def slot_table(owners, places, col_blocks, row_blocks):
    count = owners.shape[0]
    ids = jnp.arange(count, dtype=jnp.int32)
    rows = places // col_blocks
    cols = owners * col_blocks + places % col_blocks
    key = rows * count + ids
    rank = jnp.sum((key[None, :] < key[:, None]).astype(jnp.int32), axis=1)
    chosen = (rank[None, :] == ids[:, None]).astype(jnp.int32)
    code = jnp.sum(chosen * (cols * count + ids)[None, :], axis=1)
    row_at = jnp.sum(chosen * rows[None, :], axis=1)
    first = jnp.concatenate(
        [jnp.ones((1,), jnp.int32), (row_at[1:] != row_at[:-1]).astype(jnp.int32)]
    )
    targets = jnp.arange(row_blocks, dtype=jnp.int32)
    upto = jnp.sum((rows[None, :] <= targets[:, None]).astype(jnp.int32), axis=1)
    some = jnp.any(rows[None, :] == targets[:, None], axis=1)
    last = jnp.where(some, upto, 0)
    lines = [jnp.pad(v, (0, 128 - v.shape[0])) for v in (code, first, last)]
    return jnp.stack(lines + [jnp.zeros((128,), jnp.int32)] * 5)


def panel_kernel(
    cfg,
    blocks_ref, table_ref, panel_ref,
    squares_ref, totals_ref,
    pan0, pan1, own_blocks, sib_blocks, own_table, sib_table, sib_table_vmem,
    run, part0, part1, arrive0, arrive1, sib_in, sib_out, mine, stats,
    local_sem, pair_send, pair_recv,
    za_send, za_recv, zb_send, zb_recv,
    xa_send, xa_recv, ra_send, ra_recv,
    xb_send, xb_recv, rb_send, rb_recv,
    rs_send, rs_recv, out_send, out_recv, st_send, st_recv,
):
    R, S, CB, RB, BS, width, n_a = cfg
    C = 2 * CHIPS
    slab_rows = BS // R
    group = 2 * CB
    quarter = RB // CHIPS
    own_rows = quarter // 2
    pans, parts, arrives = (pan0, pan1), (part0, part1), (arrive0, arrive1)
    z = lax.axis_index("row")
    c = lax.axis_index("col")
    q = c // 2
    k = c % 2
    qx = q + 1 - 2 * (q % 2)
    qy = lax.rem(q + 2, 4)
    qd = 3 - q
    me = z * C + c
    total_devices = R * C
    nbrs = (qx, qy)
    sent = []

    def true():
        return None

    def when(cond, f):
        if cond is None:
            f()
        else:
            pl.when(cond)(f)

    def start(mk, cond=None):
        when(cond, lambda: mk().start())
        sent.append((mk, cond))

    def remote(src, dst, s, r, dev):
        return pltpu.make_async_remote_copy(
            src_ref=src, dst_ref=dst, send_sem=s, recv_sem=r, device_id=dev, device_id_type=MESH
        )

    barrier = pltpu.get_barrier_semaphore()

    def greet(d, carry):
        t = lax.rem(me + d, total_devices)
        pl.semaphore_signal(barrier, inc=1, device_id=(t // C, t % C), device_id_type=MESH)
        return carry

    lax.fori_loop(1, total_devices, greet, 0)

    def slab(zz):
        return pl.ds(pl.multiple_of(zz * slab_rows, slab_rows), slab_rows)

    def local(i, src, dst):
        return pltpu.make_async_copy(src, dst, local_sem.at[i])

    def panel_cols(core, j):
        return pl.ds(pl.multiple_of((core * PARTS + j) * width, width), width)

    for j in range(PARTS):
        local(
            j, panel_ref.at[:, :, panel_cols(k, j)],
            pans[j].at[q, pl.ds(k * CB, CB), slab(z)],
        ).start()
    local(2, table_ref, own_table).start()
    local(3, blocks_ref, own_blocks).start()
    pl.semaphore_wait(barrier, total_devices - 1)

    sib = (z, q * 2 + 1 - k)

    def pair_panel(j):
        return remote(
            panel_ref.at[:, :, panel_cols(1 - k, j)],
            pans[j].at[q, pl.ds(k * CB, CB), slab(z)],
            pair_send.at[j], pair_recv.at[j], sib,
        )

    for j in range(PARTS):
        start(functools.partial(pair_panel, j))

    def pair_table():
        return remote(table_ref, sib_table_vmem, pair_send.at[2], pair_recv.at[2], sib)

    def pair_blocks():
        return remote(blocks_ref, sib_blocks, pair_send.at[3], pair_recv.at[3], sib)

    start(pair_table)
    start(pair_blocks)

    def dev_q(qq):
        return (z, qq * 2 + k)

    def a_range(part):
        half = n_a // 2
        return (pl.ds(0, n_a), pl.ds(0, half), pl.ds(half, n_a - half))[part]

    def b_range(part):
        n_b = group - n_a
        half = n_b // 2
        return (pl.ds(n_a, n_b), pl.ds(n_a, half), pl.ds(n_a + half, n_b - half))[part]

    def za(j, up, d):
        shard = z - (d - 1) if up else z + (d - 1)
        view = pans[j].at[q, a_range(0), slab(jnp.clip(shard, 0, R - 1))]
        i = (j * 2 + up) * R + d - 1
        to = jnp.clip(z + 1 if up else z - 1, 0, R - 1)
        return remote(view, view, za_send.at[i], za_recv.at[i], (to, c))

    def zb(j, up, d):
        shard = z - (d - 1) if up else z + (d - 1)
        view = pans[j].at[:, b_range(0), slab(jnp.clip(shard, 0, R - 1))]
        i = (j * 2 + up) * R + d - 1
        to = jnp.clip(z + 1 if up else z - 1, 0, R - 1)
        return remote(view, view, zb_send.at[i], zb_recv.at[i], (to, c))

    def z_send_cond(up, d):
        if up:
            return jnp.logical_and(z - (d - 1) >= 0, z + 1 < R)
        return jnp.logical_and(z + (d - 1) < R, z - 1 >= 0)

    def z_recv_cond(up, d):
        return z - d >= 0 if up else z + d < R

    def z_from(up, d):
        return jnp.clip(z - d if up else z + d, 0, R - 1)

    def xa(j, n, zz):
        view = pans[j].at[q, a_range(0), slab(zz)]
        i = (j * 2 + n) * R + zz
        return remote(view, view, xa_send.at[i], xa_recv.at[i], dev_q(nbrs[n]))

    def ra(j, n, zz):
        view = pans[j].at[nbrs[n], a_range(1 + n), slab(zz)]
        i = (j * 2 + n) * R + zz
        return remote(view, view, ra_send.at[i], ra_recv.at[i], dev_q(nbrs[1 - n]))

    def xb(j, n):
        view = pans[j].at[q, b_range(0), slab(z)]
        i = j * 2 + n
        return remote(view, view, xb_send.at[i], xb_recv.at[i], dev_q(nbrs[n]))

    def rb(j, n):
        view = pans[j].at[nbrs[n], b_range(1 + n), slab(z)]
        i = j * 2 + n
        return remote(view, view, rb_send.at[i], rb_recv.at[i], dev_q(nbrs[1 - n]))

    p = functools.partial

    def gather_step(j, s):
        if s == 0:
            local(
                j, panel_ref.at[:, :, panel_cols(k, j)],
                pans[j].at[q, pl.ds(k * CB, CB), slab(z)],
            ).wait()
            pair_panel(j).wait_recv()
            for up in (1, 0):
                start(p(za, j, up, 1), z_send_cond(up, 1))
            for n in (0, 1):
                start(p(xb, j, n))
            for n in (0, 1):
                start(p(xa, j, n, z))
            return
        if s == 1:
            for n in (0, 1):
                xb(j, n).wait_recv()
                start(p(rb, j, n))
        if s == 2:
            for n in (0, 1):
                rb(j, n).wait_recv()
            for up in (1, 0):
                start(p(zb, j, up, 1), z_send_cond(up, 1))
        if s < R:
            for up in (1, 0):
                cond = z_recv_cond(up, s)
                when(cond, lambda: za(j, up, s).wait_recv())
                if s < R - 1:
                    start(p(za, j, up, s + 1), z_send_cond(up, s + 1))
                for n in (0, 1):
                    start(p(xa, j, n, z_from(up, s)), cond)
        if 1 <= s <= R:
            d = s - 1
            for up in (1, 0) if d else (1,):
                cond = z_recv_cond(up, d) if d else None
                zz = z_from(up, d)
                for n in (0, 1):
                    when(cond, lambda: xa(j, n, zz).wait_recv())
                    start(p(ra, j, n, zz), cond)
        if s >= 3:
            d = s - 2
            for up in (1, 0):
                when(z_recv_cond(up, d), lambda: zb(j, up, d).wait_recv())
                if d < R - 1:
                    start(p(zb, j, up, d + 1), z_send_cond(up, d + 1))
        if s == steps - 1:
            for zz in range(R):
                for n in (0, 1):
                    ra(j, n, zz).wait_recv()

    steps = R + 2

    def multiply(j, blocks, table, base):
        pan = pans[j]

        def turn(g, acc):
            for u in range(UNROLL):
                t = g * UNROLL + u
                code = table[0, t]
                slot = lax.rem(code, S)
                col = lax.div(code, S)
                product = jnp.dot(
                    blocks[slot], pan[lax.div(col, group), lax.rem(col, group)],
                    preferred_element_type=jnp.float32,
                )
                acc = jnp.where(table[1, t] == 1, 0.0, acc) + product
                run[base + t] = acc
            return acc

        lax.fori_loop(0, S // UNROLL, turn, jnp.zeros((BS, width), jnp.float32))

    def scatter(j, rel):
        qq = (qx, qy, qd)[rel]
        i = j * 3 + rel
        return remote(
            parts[j].at[pl.ds(qq * quarter, quarter)], arrives[j].at[rel],
            rs_send.at[i], rs_recv.at[i], dev_q(qq),
        )

    def add_rows(j):
        def row(i, carry):
            a = own_table[2, i]
            b = sib_table[2, i]
            b = jnp.where(b > 0, b + S, 0)
            parts[j][i] = run[a] + run[b]
            return carry

        lax.fori_loop(0, RB, row, 0)
        for rel in (2, 0, 1):
            start(p(scatter, j, rel))

    def pair_rows(j):
        return remote(sib_out.at[j], sib_in.at[j], out_send.at[j], out_recv.at[j], sib)

    def square(j):
        for rel in range(3):
            scatter(j, rel).wait_recv()

        def block(b, total, keep):
            value = parts[j][q * quarter + b]
            for rel in range(3):
                value = value + arrives[j][rel, b]
            value = value * value
            keep(value)
            return total + jnp.sum(value.reshape(BS // 8, 8, width), axis=0)

        total = jnp.zeros((8, width), jnp.float32)
        for i in range(own_rows):
            def keep(value):
                sib_out[j, i] = value
            total = block((1 - k) * own_rows + i, total, keep)
        start(p(pair_rows, j))
        for i in range(own_rows):
            def keep_mine(value):
                mine[j, i] = value
            total = block(k * own_rows + i, total, keep_mine)
        stats[me, j] = total

    lag = 2
    for s in range(steps):
        gather_step(0, s)
        if s >= lag:
            gather_step(1, s - lag)
    local(2, table_ref, own_table).wait()
    local(3, blocks_ref, own_blocks).wait()
    pair_table().wait_recv()
    local(4, sib_table_vmem, sib_table).start()
    run[0] = jnp.zeros((BS, width), jnp.float32)
    local(4, sib_table_vmem, sib_table).wait()
    pair_blocks().wait_recv()
    multiply(0, own_blocks, own_table, 1)
    gather_step(1, steps - 2)
    multiply(0, sib_blocks, sib_table, 1 + S)
    add_rows(0)
    gather_step(1, steps - 1)
    multiply(1, own_blocks, own_table, 1)
    multiply(1, sib_blocks, sib_table, 1 + S)
    add_rows(1)
    square(0)
    square(1)

    def stat(d):
        t = lax.rem(me + d, total_devices)
        return remote(
            stats.at[me], stats.at[me], st_send.at[t], st_recv.at[me], (t // C, t % C)
        )

    def stat_from(d):
        t = lax.rem(me + d, total_devices)
        return remote(
            stats.at[t], stats.at[t], st_send.at[t], st_recv.at[t], (t // C, t % C)
        )

    def send_stat(d, carry):
        stat(d).start()
        return carry

    lax.fori_loop(1, total_devices, send_stat, 0)

    def put(j, core, value_of):
        for i in range(own_rows):
            squares_ref[pl.ds(i * BS, BS), panel_cols(core, j)] = value_of(i)

    for j in range(PARTS):
        put(j, k, lambda i: mine[j, i])
    for j in range(PARTS):
        pair_rows(j).wait_recv()
        put(j, 1 - k, lambda i: sib_in[j, i])

    def take_stat(d, carry):
        stat_from(d).wait_recv()
        return carry

    lax.fori_loop(1, total_devices, take_stat, 0)

    def total_of(i, carry):
        return carry[0] + stats[2 * i], carry[1] + stats[2 * i + 1]

    zero = jnp.zeros((PARTS, 8, width), jnp.float32)
    even, odd = lax.fori_loop(0, total_devices // 2, total_of, (zero, zero))
    totals_ref[0] = even
    totals_ref[1] = odd

    for mk, cond in sent:
        when(cond, lambda: mk().wait_send())

    def done_stat(d, carry):
        stat(d).wait_send()
        return carry

    lax.fori_loop(1, total_devices, done_stat, 0)


def fused(blocks, owners, places, panel_matrix):
    R = lax.axis_size("row")
    C = lax.axis_size("col")
    S, BS, _ = blocks.shape
    CB, slab_rows, PW = panel_matrix.shape
    RB = CB * C // R
    width = PW // 2 // PARTS
    group = 2 * CB
    n_a = 10 * group // 16
    quarter = RB // CHIPS
    table = slot_table(owners, places, CB, RB)
    dma = lambda n: pltpu.SemaphoreType.DMA((n,))
    f32, bf16 = jnp.float32, blocks.dtype
    cfg = (R, S, CB, RB, BS, width, n_a)
    squares, totals = pl.pallas_call(
        functools.partial(panel_kernel, cfg),
        out_shape=(
            jax.ShapeDtypeStruct((quarter // 2 * BS, PW), f32),
            jax.ShapeDtypeStruct((2, PARTS, 8, width), f32),
        ),
        in_specs=[pl.BlockSpec(memory_space=pl.ANY)] * 3,
        out_specs=[pl.BlockSpec(memory_space=pltpu.VMEM)] * 2,
        scratch_shapes=[
            pltpu.VMEM((CHIPS, group, BS, width), bf16),
            pltpu.VMEM((CHIPS, group, BS, width), bf16),
            pltpu.VMEM((S, BS, BS), bf16),
            pltpu.VMEM((S, BS, BS), bf16),
            pltpu.SMEM((8, 128), jnp.int32),
            pltpu.SMEM((8, 128), jnp.int32),
            pltpu.VMEM((8, 128), jnp.int32),
            pltpu.VMEM((2 * S + 1, BS, width), f32),
            pltpu.VMEM((RB, BS, width), f32),
            pltpu.VMEM((RB, BS, width), f32),
            pltpu.VMEM((3, quarter, BS, width), f32),
            pltpu.VMEM((3, quarter, BS, width), f32),
            pltpu.VMEM((PARTS, quarter // 2, BS, width), f32),
            pltpu.VMEM((PARTS, quarter // 2, BS, width), f32),
            pltpu.VMEM((PARTS, quarter // 2, BS, width), f32),
            pltpu.VMEM((R * C, PARTS, 8, width), f32),
            dma(5), dma(4), dma(4),
            dma(PARTS * 2 * R), dma(PARTS * 2 * R), dma(PARTS * 2 * R), dma(PARTS * 2 * R),
            dma(PARTS * 2 * R), dma(PARTS * 2 * R), dma(PARTS * 2 * R), dma(PARTS * 2 * R),
            dma(PARTS * 2), dma(PARTS * 2), dma(PARTS * 2), dma(PARTS * 2),
            dma(PARTS * 3), dma(PARTS * 3), dma(PARTS), dma(PARTS), dma(R * C), dma(R * C),
        ],
        compiler_params=pltpu.CompilerParams(
            collective_id=0, has_side_effects=True, vmem_limit_bytes=48 << 20
        ),
        cost_estimate=pl.CostEstimate(
            flops=2 * S * BS * BS * PW, bytes_accessed=4 << 20, transcendentals=0
        ),
    )(blocks, table, panel_matrix)
    col_mean = jnp.sum(totals, axis=2).reshape(PW) / (CB * C * BS)
    return squares / (col_mean + epsilon)


def on_device(blocks, owners, places, panel_matrix):
    col_count = lax.axis_size("col")
    row_count = lax.axis_size("row")
    col_blocks = panel_matrix.shape[0]
    block_side = blocks.shape[1]
    panel_width = panel_matrix.shape[2]
    row_blocks = col_blocks * col_count // row_count
    capacity = row_blocks * col_blocks // col_count
    targets = jnp.arange(col_count, dtype=jnp.int32)
    onehot = (owners[:, None] == targets[None, :]).astype(jnp.int32)
    before = jnp.cumsum(onehot, axis=0) - onehot
    bucket_rank = jnp.sum(before * onehot, axis=1)
    slot_index = owners * capacity + bucket_rank
    received = col_count * capacity
    outgoing = (
        jnp.zeros((received, block_side, block_side), blocks.dtype).at[slot_index].set(blocks)
    )
    out_places = jnp.zeros((received,), jnp.int32).at[slot_index].set(places)
    outgoing = outgoing.reshape(col_count, capacity, block_side, block_side)
    out_places = out_places.reshape(col_count, capacity)
    arrived, arrived_places = (
        lax.all_to_all(outgoing, "col", split_axis=0, concat_axis=0, tiled=True),
        lax.all_to_all(out_places, "col", split_axis=0, concat_axis=0, tiled=True),
    )
    arrived = arrived.reshape(received, block_side, block_side)
    arrived_places = arrived_places.reshape(received)
    row_in = arrived_places // col_blocks
    col_in = arrived_places % col_blocks
    panel_full = lax.all_gather(panel_matrix, "row", axis=1, tiled=True)
    group_size = min(32, received)
    turn_count = received // group_size

    def add_group(partial_value, members):
        tile_group, group_rows, group_cols = members
        pieces = panel_full[group_cols]
        product = jnp.einsum("sab,sbp->sap", tile_group, pieces, preferred_element_type=jnp.float32)
        return (partial_value.at[group_rows].add(product), None)

    start_sum = jnp.zeros((row_blocks, block_side, panel_width), jnp.float32)
    partial_value = lax.scan(
        add_group,
        start_sum,
        (
            arrived.reshape(turn_count, group_size, block_side, block_side),
            row_in.reshape(turn_count, group_size),
            col_in.reshape(turn_count, group_size),
        ),
    )[0]
    partial_rows = partial_value.reshape(row_blocks * block_side, panel_width)
    own_rows = lax.psum_scatter(partial_rows, "col", scatter_dimension=0, tiled=True)
    squares = own_rows * own_rows
    totals = lax.psum(jnp.sum(squares, axis=0), ("row", "col"))
    col_mean = totals / (col_blocks * col_count * block_side)
    return squares / (col_mean + epsilon)


def solution(mesh):
    fits = mesh.shape["col"] == 2 * CHIPS and mesh.shape["row"] == 4
    placed = (
        P(("row", "col"), None, None),
        P(("row", "col")),
        P(("row", "col")),
        P("col", "row", None),
    )
    return jax.shard_map(
        fused if fits else on_device, mesh=mesh, in_specs=placed, out_specs=P(("row", "col"), None), check_vma=False
    )
```

```python
import functools

import jax
import jax.numpy as jnp
from jax import lax
from jax.experimental import pallas as pl
from jax.experimental.pallas import tpu as pltpu
from jax.sharding import PartitionSpec as P

epsilon = 1e-06
CHIPS = 4
PARTS = 2
UNROLL = 8
MESH = pl.DeviceIdType.MESH


def slot_table(owners, places, col_blocks, row_blocks):
    count = owners.shape[0]
    ids = jnp.arange(count, dtype=jnp.int32)
    rows = places // col_blocks
    cols = owners * col_blocks + places % col_blocks
    key = rows * count + ids
    rank = jnp.sum((key[None, :] < key[:, None]).astype(jnp.int32), axis=1)
    chosen = (rank[None, :] == ids[:, None]).astype(jnp.int32)
    code = jnp.sum(chosen * (cols * count + ids)[None, :], axis=1)
    row_at = jnp.sum(chosen * rows[None, :], axis=1)
    first = jnp.concatenate(
        [jnp.ones((1,), jnp.int32), (row_at[1:] != row_at[:-1]).astype(jnp.int32)]
    )
    targets = jnp.arange(row_blocks, dtype=jnp.int32)
    upto = jnp.sum((rows[None, :] <= targets[:, None]).astype(jnp.int32), axis=1)
    some = jnp.any(rows[None, :] == targets[:, None], axis=1)
    last = jnp.where(some, upto, 0)
    lines = [jnp.pad(v, (0, 128 - v.shape[0])) for v in (code, first, last)]
    return jnp.stack(lines + [jnp.zeros((128,), jnp.int32)] * 5)


def panel_kernel(
    cfg,
    blocks_ref, table_ref, panel_ref,
    squares_ref, totals_ref,
    pan0, pan1, own_blocks, sib_blocks, own_table, sib_table, sib_table_vmem,
    run, part0, part1, arrive0, arrive1, sib_in, sib_out, mine, stats,
    local_sem, pair_send, pair_recv,
    za_send, za_recv, zb_send, zb_recv,
    xa_send, xa_recv, ra_send, ra_recv,
    xb_send, xb_recv, rb_send, rb_recv,
    rs_send, rs_recv, out_send, out_recv, st_send, st_recv,
):
    R, S, CB, RB, BS, width, n_a = cfg
    C = 2 * CHIPS
    slab_rows = BS // R
    group = 2 * CB
    quarter = RB // CHIPS
    own_rows = quarter // 2
    pans, parts, arrives = (pan0, pan1), (part0, part1), (arrive0, arrive1)
    z = lax.axis_index("row")
    c = lax.axis_index("col")
    q = c // 2
    k = c % 2
    qx = q + 1 - 2 * (q % 2)
    qy = lax.rem(q + 2, 4)
    qd = 3 - q
    me = z * C + c
    total_devices = R * C
    nbrs = (qx, qy)
    sent = []

    def true():
        return None

    def when(cond, f):
        if cond is None:
            f()
        else:
            pl.when(cond)(f)

    def start(mk, cond=None):
        when(cond, lambda: mk().start())
        sent.append((mk, cond))

    def remote(src, dst, s, r, dev):
        return pltpu.make_async_remote_copy(
            src_ref=src, dst_ref=dst, send_sem=s, recv_sem=r, device_id=dev, device_id_type=MESH
        )

    barrier = pltpu.get_barrier_semaphore()

    def greet(d, carry):
        t = lax.rem(me + d, total_devices)
        pl.semaphore_signal(barrier, inc=1, device_id=(t // C, t % C), device_id_type=MESH)
        return carry

    lax.fori_loop(1, total_devices, greet, 0)

    def slab(zz):
        return pl.ds(pl.multiple_of(zz * slab_rows, slab_rows), slab_rows)

    def local(i, src, dst):
        return pltpu.make_async_copy(src, dst, local_sem.at[i])

    def panel_cols(core, j):
        return pl.ds(pl.multiple_of((core * PARTS + j) * width, width), width)

    for j in range(PARTS):
        local(
            j, panel_ref.at[:, :, panel_cols(k, j)],
            pans[j].at[q, pl.ds(k * CB, CB), slab(z)],
        ).start()
    local(2, table_ref, own_table).start()
    local(3, blocks_ref, own_blocks).start()
    pl.semaphore_wait(barrier, total_devices - 1)

    sib = (z, q * 2 + 1 - k)

    def pair_panel(j):
        return remote(
            panel_ref.at[:, :, panel_cols(1 - k, j)],
            pans[j].at[q, pl.ds(k * CB, CB), slab(z)],
            pair_send.at[j], pair_recv.at[j], sib,
        )

    for j in range(PARTS):
        start(functools.partial(pair_panel, j))

    def pair_table():
        return remote(table_ref, sib_table_vmem, pair_send.at[2], pair_recv.at[2], sib)

    def pair_blocks():
        return remote(blocks_ref, sib_blocks, pair_send.at[3], pair_recv.at[3], sib)

    start(pair_table)
    start(pair_blocks)

    def dev_q(qq):
        return (z, qq * 2 + k)

    def a_range(part):
        half = n_a // 2
        return (pl.ds(0, n_a), pl.ds(0, half), pl.ds(half, n_a - half))[part]

    def b_range(part):
        n_b = group - n_a
        half = n_b // 2
        return (pl.ds(n_a, n_b), pl.ds(n_a, half), pl.ds(n_a + half, n_b - half))[part]

    def za(j, up, d):
        shard = z - (d - 1) if up else z + (d - 1)
        view = pans[j].at[q, a_range(0), slab(jnp.clip(shard, 0, R - 1))]
        i = (j * 2 + up) * R + d - 1
        to = jnp.clip(z + 1 if up else z - 1, 0, R - 1)
        return remote(view, view, za_send.at[i], za_recv.at[i], (to, c))

    def zb(j, up, d):
        shard = z - (d - 1) if up else z + (d - 1)
        view = pans[j].at[:, b_range(0), slab(jnp.clip(shard, 0, R - 1))]
        i = (j * 2 + up) * R + d - 1
        to = jnp.clip(z + 1 if up else z - 1, 0, R - 1)
        return remote(view, view, zb_send.at[i], zb_recv.at[i], (to, c))

    def z_send_cond(up, d):
        if up:
            return jnp.logical_and(z - (d - 1) >= 0, z + 1 < R)
        return jnp.logical_and(z + (d - 1) < R, z - 1 >= 0)

    def z_recv_cond(up, d):
        return z - d >= 0 if up else z + d < R

    def z_from(up, d):
        return jnp.clip(z - d if up else z + d, 0, R - 1)

    def xa(j, n, zz):
        view = pans[j].at[q, a_range(0), slab(zz)]
        i = (j * 2 + n) * R + zz
        return remote(view, view, xa_send.at[i], xa_recv.at[i], dev_q(nbrs[n]))

    def ra(j, n, zz):
        view = pans[j].at[nbrs[n], a_range(1 + n), slab(zz)]
        i = (j * 2 + n) * R + zz
        return remote(view, view, ra_send.at[i], ra_recv.at[i], dev_q(nbrs[1 - n]))

    def xb(j, n):
        view = pans[j].at[q, b_range(0), slab(z)]
        i = j * 2 + n
        return remote(view, view, xb_send.at[i], xb_recv.at[i], dev_q(nbrs[n]))

    def rb(j, n):
        view = pans[j].at[nbrs[n], b_range(1 + n), slab(z)]
        i = j * 2 + n
        return remote(view, view, rb_send.at[i], rb_recv.at[i], dev_q(nbrs[1 - n]))

    p = functools.partial

    def gather_step(j, s):
        if s == 0:
            local(
                j, panel_ref.at[:, :, panel_cols(k, j)],
                pans[j].at[q, pl.ds(k * CB, CB), slab(z)],
            ).wait()
            pair_panel(j).wait_recv()
            for up in (1, 0):
                start(p(za, j, up, 1), z_send_cond(up, 1))
            for n in (0, 1):
                start(p(xb, j, n))
            for n in (0, 1):
                start(p(xa, j, n, z))
            return
        if s == 1:
            for n in (0, 1):
                xb(j, n).wait_recv()
                start(p(rb, j, n))
        if s == 2:
            for n in (0, 1):
                rb(j, n).wait_recv()
            for up in (1, 0):
                start(p(zb, j, up, 1), z_send_cond(up, 1))
        if s < R:
            for up in (1, 0):
                cond = z_recv_cond(up, s)
                when(cond, lambda: za(j, up, s).wait_recv())
                if s < R - 1:
                    start(p(za, j, up, s + 1), z_send_cond(up, s + 1))
                for n in (0, 1):
                    start(p(xa, j, n, z_from(up, s)), cond)
        if 1 <= s <= R:
            d = s - 1
            for up in (1, 0) if d else (1,):
                cond = z_recv_cond(up, d) if d else None
                zz = z_from(up, d)
                for n in (0, 1):
                    when(cond, lambda: xa(j, n, zz).wait_recv())
                    start(p(ra, j, n, zz), cond)
        if s >= 3:
            d = s - 2
            for up in (1, 0):
                when(z_recv_cond(up, d), lambda: zb(j, up, d).wait_recv())
                if d < R - 1:
                    start(p(zb, j, up, d + 1), z_send_cond(up, d + 1))
        if s == steps - 1:
            for zz in range(R):
                for n in (0, 1):
                    ra(j, n, zz).wait_recv()

    steps = R + 2

    def multiply(j, blocks, table, base):
        pan = pans[j]

        def turn(g, acc):
            for u in range(UNROLL):
                t = g * UNROLL + u
                code = table[0, t]
                slot = lax.rem(code, S)
                col = lax.div(code, S)
                product = jnp.dot(
                    blocks[slot], pan[lax.div(col, group), lax.rem(col, group)],
                    preferred_element_type=jnp.float32,
                )
                acc = jnp.where(table[1, t] == 1, 0.0, acc) + product
                run[base + t] = acc
            return acc

        lax.fori_loop(0, S // UNROLL, turn, jnp.zeros((BS, width), jnp.float32))

    def scatter(j, rel):
        qq = (qx, qy, qd)[rel]
        i = j * 3 + rel
        return remote(
            parts[j].at[pl.ds(qq * quarter, quarter)], arrives[j].at[rel],
            rs_send.at[i], rs_recv.at[i], dev_q(qq),
        )

    def add_rows(j):
        def row(i, carry):
            a = own_table[2, i]
            b = sib_table[2, i]
            b = jnp.where(b > 0, b + S, 0)
            parts[j][i] = run[a] + run[b]
            return carry

        lax.fori_loop(0, RB, row, 0)
        for rel in (2, 0, 1):
            start(p(scatter, j, rel))

    def pair_rows(j):
        return remote(sib_out.at[j], sib_in.at[j], out_send.at[j], out_recv.at[j], sib)

    def square(j):
        for rel in range(3):
            scatter(j, rel).wait_recv()

        def block(b, total, keep):
            value = parts[j][q * quarter + b]
            for rel in range(3):
                value = value + arrives[j][rel, b]
            value = value * value
            keep(value)
            return total + jnp.sum(value.reshape(BS // 8, 8, width), axis=0)

        total = jnp.zeros((8, width), jnp.float32)
        for i in range(own_rows):
            def keep(value):
                sib_out[j, i] = value
            total = block((1 - k) * own_rows + i, total, keep)
        start(p(pair_rows, j))
        for i in range(own_rows):
            def keep_mine(value):
                mine[j, i] = value
            total = block(k * own_rows + i, total, keep_mine)
        stats[me, pl.ds(j, 1)] = jnp.sum(total, axis=0, keepdims=True)

    lag = 2
    for s in range(steps):
        gather_step(0, s)
        if s >= lag:
            gather_step(1, s - lag)
    local(2, table_ref, own_table).wait()
    local(3, blocks_ref, own_blocks).wait()
    pair_table().wait_recv()
    local(4, sib_table_vmem, sib_table).start()
    run[0] = jnp.zeros((BS, width), jnp.float32)
    local(4, sib_table_vmem, sib_table).wait()
    pair_blocks().wait_recv()
    multiply(0, own_blocks, own_table, 1)
    gather_step(1, steps - 2)
    multiply(0, sib_blocks, sib_table, 1 + S)
    add_rows(0)
    gather_step(1, steps - 1)
    multiply(1, own_blocks, own_table, 1)
    multiply(1, sib_blocks, sib_table, 1 + S)
    add_rows(1)
    square(0)
    square(1)

    def stat(d):
        t = lax.rem(me + d, total_devices)
        return remote(
            stats.at[me], stats.at[me], st_send.at[t], st_recv.at[me], (t // C, t % C)
        )

    def stat_from(d):
        t = lax.rem(me + d, total_devices)
        return remote(
            stats.at[t], stats.at[t], st_send.at[t], st_recv.at[t], (t // C, t % C)
        )

    def send_stat(d, carry):
        stat(d).start()
        return carry

    lax.fori_loop(1, total_devices, send_stat, 0)

    def put(j, core, value_of):
        for i in range(own_rows):
            squares_ref[pl.ds(i * BS, BS), panel_cols(core, j)] = value_of(i)

    for j in range(PARTS):
        put(j, k, lambda i: mine[j, i])
    for j in range(PARTS):
        pair_rows(j).wait_recv()
        put(j, 1 - k, lambda i: sib_in[j, i])

    def take_stat(d, carry):
        stat_from(d).wait_recv()
        return carry

    lax.fori_loop(1, total_devices, take_stat, 0)

    def total_of(i, carry):
        return carry[0] + stats[2 * i], carry[1] + stats[2 * i + 1]

    zero = jnp.zeros((PARTS, width), jnp.float32)
    even, odd = lax.fori_loop(0, total_devices // 2, total_of, (zero, zero))
    totals_ref[0] = even
    totals_ref[1] = odd

    for mk, cond in sent:
        when(cond, lambda: mk().wait_send())

    def done_stat(d, carry):
        stat(d).wait_send()
        return carry

    lax.fori_loop(1, total_devices, done_stat, 0)


def fused(blocks, owners, places, panel_matrix):
    R = lax.axis_size("row")
    C = lax.axis_size("col")
    S, BS, _ = blocks.shape
    CB, slab_rows, PW = panel_matrix.shape
    RB = CB * C // R
    width = PW // 2 // PARTS
    group = 2 * CB
    n_a = 12 * group // 16
    quarter = RB // CHIPS
    table = slot_table(owners, places, CB, RB)
    dma = lambda n: pltpu.SemaphoreType.DMA((n,))
    f32, bf16 = jnp.float32, blocks.dtype
    cfg = (R, S, CB, RB, BS, width, n_a)
    squares, totals = pl.pallas_call(
        functools.partial(panel_kernel, cfg),
        out_shape=(
            jax.ShapeDtypeStruct((quarter // 2 * BS, PW), f32),
            jax.ShapeDtypeStruct((2, PARTS, width), f32),
        ),
        in_specs=[pl.BlockSpec(memory_space=pl.ANY)] * 3,
        out_specs=[pl.BlockSpec(memory_space=pltpu.VMEM)] * 2,
        scratch_shapes=[
            pltpu.VMEM((CHIPS, group, BS, width), bf16),
            pltpu.VMEM((CHIPS, group, BS, width), bf16),
            pltpu.VMEM((S, BS, BS), bf16),
            pltpu.VMEM((S, BS, BS), bf16),
            pltpu.SMEM((8, 128), jnp.int32),
            pltpu.SMEM((8, 128), jnp.int32),
            pltpu.VMEM((8, 128), jnp.int32),
            pltpu.VMEM((2 * S + 1, BS, width), f32),
            pltpu.VMEM((RB, BS, width), f32),
            pltpu.VMEM((RB, BS, width), f32),
            pltpu.VMEM((3, quarter, BS, width), f32),
            pltpu.VMEM((3, quarter, BS, width), f32),
            pltpu.VMEM((PARTS, quarter // 2, BS, width), f32),
            pltpu.VMEM((PARTS, quarter // 2, BS, width), f32),
            pltpu.VMEM((PARTS, quarter // 2, BS, width), f32),
            pltpu.VMEM((R * C, PARTS, width), f32),
            dma(5), dma(4), dma(4),
            dma(PARTS * 2 * R), dma(PARTS * 2 * R), dma(PARTS * 2 * R), dma(PARTS * 2 * R),
            dma(PARTS * 2 * R), dma(PARTS * 2 * R), dma(PARTS * 2 * R), dma(PARTS * 2 * R),
            dma(PARTS * 2), dma(PARTS * 2), dma(PARTS * 2), dma(PARTS * 2),
            dma(PARTS * 3), dma(PARTS * 3), dma(PARTS), dma(PARTS), dma(R * C), dma(R * C),
        ],
        compiler_params=pltpu.CompilerParams(
            collective_id=0, has_side_effects=True, vmem_limit_bytes=60 << 20
        ),
        cost_estimate=pl.CostEstimate(
            flops=2 * S * BS * BS * PW, bytes_accessed=4 << 20, transcendentals=0
        ),
    )(blocks, table, panel_matrix)
    col_mean = totals.reshape(PW) / (CB * C * BS)
    return squares / (col_mean + epsilon)


def on_device(blocks, owners, places, panel_matrix):
    col_count = lax.axis_size("col")
    row_count = lax.axis_size("row")
    col_blocks = panel_matrix.shape[0]
    block_side = blocks.shape[1]
    panel_width = panel_matrix.shape[2]
    row_blocks = col_blocks * col_count // row_count
    capacity = row_blocks * col_blocks // col_count
    targets = jnp.arange(col_count, dtype=jnp.int32)
    onehot = (owners[:, None] == targets[None, :]).astype(jnp.int32)
    before = jnp.cumsum(onehot, axis=0) - onehot
    bucket_rank = jnp.sum(before * onehot, axis=1)
    slot_index = owners * capacity + bucket_rank
    received = col_count * capacity
    outgoing = (
        jnp.zeros((received, block_side, block_side), blocks.dtype).at[slot_index].set(blocks)
    )
    out_places = jnp.zeros((received,), jnp.int32).at[slot_index].set(places)
    outgoing = outgoing.reshape(col_count, capacity, block_side, block_side)
    out_places = out_places.reshape(col_count, capacity)
    arrived, arrived_places = (
        lax.all_to_all(outgoing, "col", split_axis=0, concat_axis=0, tiled=True),
        lax.all_to_all(out_places, "col", split_axis=0, concat_axis=0, tiled=True),
    )
    arrived = arrived.reshape(received, block_side, block_side)
    arrived_places = arrived_places.reshape(received)
    row_in = arrived_places // col_blocks
    col_in = arrived_places % col_blocks
    panel_full = lax.all_gather(panel_matrix, "row", axis=1, tiled=True)
    group_size = min(32, received)
    turn_count = received // group_size

    def add_group(partial_value, members):
        tile_group, group_rows, group_cols = members
        pieces = panel_full[group_cols]
        product = jnp.einsum("sab,sbp->sap", tile_group, pieces, preferred_element_type=jnp.float32)
        return (partial_value.at[group_rows].add(product), None)

    start_sum = jnp.zeros((row_blocks, block_side, panel_width), jnp.float32)
    partial_value = lax.scan(
        add_group,
        start_sum,
        (
            arrived.reshape(turn_count, group_size, block_side, block_side),
            row_in.reshape(turn_count, group_size),
            col_in.reshape(turn_count, group_size),
        ),
    )[0]
    partial_rows = partial_value.reshape(row_blocks * block_side, panel_width)
    own_rows = lax.psum_scatter(partial_rows, "col", scatter_dimension=0, tiled=True)
    squares = own_rows * own_rows
    totals = lax.psum(jnp.sum(squares, axis=0), ("row", "col"))
    col_mean = totals / (col_blocks * col_count * block_side)
    return squares / (col_mean + epsilon)


def solution(mesh):
    fits = mesh.shape["col"] == 2 * CHIPS and mesh.shape["row"] == 4
    placed = (
        P(("row", "col"), None, None),
        P(("row", "col")),
        P(("row", "col")),
        P("col", "row", None),
    )
    return jax.shard_map(
        fused if fits else on_device, mesh=mesh, in_specs=placed, out_specs=P(("row", "col"), None), check_vma=False
    )
```

```python
import functools

import jax
import jax.numpy as jnp
from jax import lax
from jax.experimental import pallas as pl
from jax.experimental.pallas import tpu as pltpu
from jax.sharding import PartitionSpec as P

epsilon = 1e-06
CHIPS = 4
PARTS = 2
UNROLL = 8
LEVELS = 32767.0
smallest = 1e-30
MESH = pl.DeviceIdType.MESH


def slot_table(owners, places, col_blocks, row_blocks):
    count = owners.shape[0]
    ids = jnp.arange(count, dtype=jnp.int32)
    rows = places // col_blocks
    cols = owners * col_blocks + places % col_blocks
    key = rows * count + ids
    rank = jnp.sum((key[None, :] < key[:, None]).astype(jnp.int32), axis=1)
    chosen = (rank[None, :] == ids[:, None]).astype(jnp.int32)
    code = jnp.sum(chosen * (cols * count + ids)[None, :], axis=1)
    row_at = jnp.sum(chosen * rows[None, :], axis=1)
    first = jnp.concatenate(
        [jnp.ones((1,), jnp.int32), (row_at[1:] != row_at[:-1]).astype(jnp.int32)]
    )
    targets = jnp.arange(row_blocks, dtype=jnp.int32)
    upto = jnp.sum((rows[None, :] <= targets[:, None]).astype(jnp.int32), axis=1)
    some = jnp.any(rows[None, :] == targets[:, None], axis=1)
    last = jnp.where(some, upto, 0)
    lines = [jnp.pad(v, (0, 128 - v.shape[0])) for v in (code, first, last)]
    return jnp.stack(lines + [jnp.zeros((128,), jnp.int32)] * 5)


def panel_kernel(
    cfg,
    blocks_ref, table_ref, panel_ref,
    squares_ref, totals_ref,
    pan0, pan1, own_blocks, sib_blocks, own_table, sib_table, sib_table_vmem,
    run, part, code0, code1, arrive0, arrive1, scale_out, scale_in, sib_in, sib_out, mine, stats,
    local_sem, pair_send, pair_recv,
    za_send, za_recv, zb_send, zb_recv,
    xa_send, xa_recv, ra_send, ra_recv,
    xb_send, xb_recv, rb_send, rb_recv,
    rs_send, rs_recv, sc_send, sc_recv, out_send, out_recv, st_send, st_recv,
):
    R, S, CB, RB, BS, width, n_a = cfg
    C = 2 * CHIPS
    slab_rows = BS // R
    group = 2 * CB
    quarter = RB // CHIPS
    own_rows = quarter // 2
    pans, codes, arrives = (pan0, pan1), (code0, code1), (arrive0, arrive1)
    z = lax.axis_index("row")
    c = lax.axis_index("col")
    q = c // 2
    k = c % 2
    qx = q + 1 - 2 * (q % 2)
    qy = lax.rem(q + 2, 4)
    qd = 3 - q
    me = z * C + c
    total_devices = R * C
    nbrs = (qx, qy)
    sent = []

    def true():
        return None

    def when(cond, f):
        if cond is None:
            f()
        else:
            pl.when(cond)(f)

    def start(mk, cond=None):
        when(cond, lambda: mk().start())
        sent.append((mk, cond))

    def remote(src, dst, s, r, dev):
        return pltpu.make_async_remote_copy(
            src_ref=src, dst_ref=dst, send_sem=s, recv_sem=r, device_id=dev, device_id_type=MESH
        )

    barrier = pltpu.get_barrier_semaphore()

    def greet(d, carry):
        t = lax.rem(me + d, total_devices)
        pl.semaphore_signal(barrier, inc=1, device_id=(t // C, t % C), device_id_type=MESH)
        return carry

    lax.fori_loop(1, total_devices, greet, 0)

    def slab(zz):
        return pl.ds(pl.multiple_of(zz * slab_rows, slab_rows), slab_rows)

    def local(i, src, dst):
        return pltpu.make_async_copy(src, dst, local_sem.at[i])

    def panel_cols(core, j):
        return pl.ds(pl.multiple_of((core * PARTS + j) * width, width), width)

    for j in range(PARTS):
        local(
            j, panel_ref.at[:, :, panel_cols(k, j)],
            pans[j].at[q, pl.ds(k * CB, CB), slab(z)],
        ).start()
    local(2, table_ref, own_table).start()
    local(3, blocks_ref, own_blocks).start()
    pl.semaphore_wait(barrier, total_devices - 1)

    sib = (z, q * 2 + 1 - k)

    def pair_panel(j):
        return remote(
            panel_ref.at[:, :, panel_cols(1 - k, j)],
            pans[j].at[q, pl.ds(k * CB, CB), slab(z)],
            pair_send.at[j], pair_recv.at[j], sib,
        )

    for j in range(PARTS):
        start(functools.partial(pair_panel, j))

    def pair_table():
        return remote(table_ref, sib_table_vmem, pair_send.at[2], pair_recv.at[2], sib)

    def pair_blocks():
        return remote(blocks_ref, sib_blocks, pair_send.at[3], pair_recv.at[3], sib)

    start(pair_table)
    start(pair_blocks)

    def dev_q(qq):
        return (z, qq * 2 + k)

    def a_range(part):
        half = n_a // 2
        return (pl.ds(0, n_a), pl.ds(0, half), pl.ds(half, n_a - half))[part]

    def b_range(part):
        n_b = group - n_a
        half = n_b // 2
        return (pl.ds(n_a, n_b), pl.ds(n_a, half), pl.ds(n_a + half, n_b - half))[part]

    def za(j, up, d):
        shard = z - (d - 1) if up else z + (d - 1)
        view = pans[j].at[q, a_range(0), slab(jnp.clip(shard, 0, R - 1))]
        i = (j * 2 + up) * R + d - 1
        to = jnp.clip(z + 1 if up else z - 1, 0, R - 1)
        return remote(view, view, za_send.at[i], za_recv.at[i], (to, c))

    def zb(j, up, d):
        shard = z - (d - 1) if up else z + (d - 1)
        view = pans[j].at[:, b_range(0), slab(jnp.clip(shard, 0, R - 1))]
        i = (j * 2 + up) * R + d - 1
        to = jnp.clip(z + 1 if up else z - 1, 0, R - 1)
        return remote(view, view, zb_send.at[i], zb_recv.at[i], (to, c))

    def z_send_cond(up, d):
        if up:
            return jnp.logical_and(z - (d - 1) >= 0, z + 1 < R)
        return jnp.logical_and(z + (d - 1) < R, z - 1 >= 0)

    def z_recv_cond(up, d):
        return z - d >= 0 if up else z + d < R

    def z_from(up, d):
        return jnp.clip(z - d if up else z + d, 0, R - 1)

    def xa(j, n, zz):
        view = pans[j].at[q, a_range(0), slab(zz)]
        i = (j * 2 + n) * R + zz
        return remote(view, view, xa_send.at[i], xa_recv.at[i], dev_q(nbrs[n]))

    def ra(j, n, zz):
        view = pans[j].at[nbrs[n], a_range(1 + n), slab(zz)]
        i = (j * 2 + n) * R + zz
        return remote(view, view, ra_send.at[i], ra_recv.at[i], dev_q(nbrs[1 - n]))

    def xb(j, n):
        view = pans[j].at[q, b_range(0), slab(z)]
        i = j * 2 + n
        return remote(view, view, xb_send.at[i], xb_recv.at[i], dev_q(nbrs[n]))

    def rb(j, n):
        view = pans[j].at[nbrs[n], b_range(1 + n), slab(z)]
        i = j * 2 + n
        return remote(view, view, rb_send.at[i], rb_recv.at[i], dev_q(nbrs[1 - n]))

    p = functools.partial

    def gather_step(j, s):
        if s == 0:
            local(
                j, panel_ref.at[:, :, panel_cols(k, j)],
                pans[j].at[q, pl.ds(k * CB, CB), slab(z)],
            ).wait()
            pair_panel(j).wait_recv()
            for up in (1, 0):
                start(p(za, j, up, 1), z_send_cond(up, 1))
            for n in (0, 1):
                start(p(xb, j, n))
            for n in (0, 1):
                start(p(xa, j, n, z))
            return
        if s == 1:
            for n in (0, 1):
                xb(j, n).wait_recv()
                start(p(rb, j, n))
        if s == 2:
            for n in (0, 1):
                rb(j, n).wait_recv()
            for up in (1, 0):
                start(p(zb, j, up, 1), z_send_cond(up, 1))
        if s < R:
            for up in (1, 0):
                cond = z_recv_cond(up, s)
                when(cond, lambda: za(j, up, s).wait_recv())
                if s < R - 1:
                    start(p(za, j, up, s + 1), z_send_cond(up, s + 1))
                for n in (0, 1):
                    start(p(xa, j, n, z_from(up, s)), cond)
        if 1 <= s <= R:
            d = s - 1
            for up in (1, 0) if d else (1,):
                cond = z_recv_cond(up, d) if d else None
                zz = z_from(up, d)
                for n in (0, 1):
                    when(cond, lambda: xa(j, n, zz).wait_recv())
                    start(p(ra, j, n, zz), cond)
        if s >= 3:
            d = s - 2
            for up in (1, 0):
                when(z_recv_cond(up, d), lambda: zb(j, up, d).wait_recv())
                if d < R - 1:
                    start(p(zb, j, up, d + 1), z_send_cond(up, d + 1))
        if s == steps - 1:
            for zz in range(R):
                for n in (0, 1):
                    ra(j, n, zz).wait_recv()

    steps = R + 2

    def multiply(j, blocks, table, base):
        pan = pans[j]

        def turn(g, acc):
            for u in range(UNROLL):
                t = g * UNROLL + u
                code = table[0, t]
                slot = lax.rem(code, S)
                col = lax.div(code, S)
                product = jnp.dot(
                    blocks[slot], pan[lax.div(col, group), lax.rem(col, group)],
                    preferred_element_type=jnp.float32,
                )
                acc = jnp.where(table[1, t] == 1, 0.0, acc) + product
                run[base + t] = acc
            return acc

        lax.fori_loop(0, S // UNROLL, turn, jnp.zeros((BS, width), jnp.float32))

    others = (qx, qy, qd)

    def scatter(j, rel):
        i = j * 3 + rel
        return remote(
            codes[j].at[rel], arrives[j].at[rel], rs_send.at[i], rs_recv.at[i],
            dev_q(others[rel]),
        )

    def scatter_scale(j, rel):
        i = j * 3 + rel
        return remote(
            scale_out.at[i], scale_in.at[i], sc_send.at[i], sc_recv.at[i], dev_q(others[rel])
        )

    def row_sum(i):
        a = own_table[2, i]
        b = sib_table[2, i]
        b = jnp.where(b > 0, b + S, 0)
        return run[a] + run[b]

    def add_rows(j):
        for rel in (2, 0, 1):
            for b in range(quarter):
                value = row_sum(others[rel] * quarter + b)
                top = jnp.max(jnp.abs(value), axis=0, keepdims=True)
                top = jnp.maximum(top, smallest)
                codes[j][rel, b] = jnp.round(value * (LEVELS / top)).astype(jnp.int32).astype(jnp.int16)
                scale_out[j * 3 + rel, pl.ds(b, 1)] = top * (1.0 / LEVELS)
            start(p(scatter_scale, j, rel))
            start(p(scatter, j, rel))
        for b in range(quarter):
            part[j, b] = row_sum(q * quarter + b)

    def pair_rows(j):
        return remote(sib_out.at[j], sib_in.at[j], out_send.at[j], out_recv.at[j], sib)

    def square(j):
        for rel in range(3):
            scatter_scale(j, rel).wait_recv()
            scatter(j, rel).wait_recv()

        def block(b, total, keep):
            value = part[j, b]
            for rel in range(3):
                code = arrives[j][rel, b].astype(jnp.int32).astype(jnp.float32)
                value = value + code * scale_in[j * 3 + rel, pl.ds(b, 1)]
            value = value * value
            keep(value)
            return total + jnp.sum(value.reshape(BS // 8, 8, width), axis=0)

        total = jnp.zeros((8, width), jnp.float32)
        for i in range(own_rows):
            def keep(value):
                sib_out[j, i] = value
            total = block((1 - k) * own_rows + i, total, keep)
        start(p(pair_rows, j))
        for i in range(own_rows):
            def keep_mine(value):
                mine[j, i] = value
            total = block(k * own_rows + i, total, keep_mine)
        stats[me, pl.ds(j, 1)] = jnp.sum(total, axis=0, keepdims=True)

    lag = 2
    for s in range(steps):
        gather_step(0, s)
        if s >= lag:
            gather_step(1, s - lag)
    local(2, table_ref, own_table).wait()
    local(3, blocks_ref, own_blocks).wait()
    pair_table().wait_recv()
    local(4, sib_table_vmem, sib_table).start()
    run[0] = jnp.zeros((BS, width), jnp.float32)
    local(4, sib_table_vmem, sib_table).wait()
    pair_blocks().wait_recv()
    multiply(0, own_blocks, own_table, 1)
    gather_step(1, steps - 2)
    multiply(0, sib_blocks, sib_table, 1 + S)
    add_rows(0)
    gather_step(1, steps - 1)
    multiply(1, own_blocks, own_table, 1)
    multiply(1, sib_blocks, sib_table, 1 + S)
    add_rows(1)
    square(0)
    square(1)

    def stat(d):
        t = lax.rem(me + d, total_devices)
        return remote(
            stats.at[me], stats.at[me], st_send.at[t], st_recv.at[me], (t // C, t % C)
        )

    def stat_from(d):
        t = lax.rem(me + d, total_devices)
        return remote(
            stats.at[t], stats.at[t], st_send.at[t], st_recv.at[t], (t // C, t % C)
        )

    def send_stat(d, carry):
        stat(d).start()
        return carry

    lax.fori_loop(1, total_devices, send_stat, 0)

    def put(j, core, value_of):
        for i in range(own_rows):
            squares_ref[pl.ds(i * BS, BS), panel_cols(core, j)] = value_of(i)

    for j in range(PARTS):
        put(j, k, lambda i: mine[j, i])
    for j in range(PARTS):
        pair_rows(j).wait_recv()
        put(j, 1 - k, lambda i: sib_in[j, i])

    def take_stat(d, carry):
        stat_from(d).wait_recv()
        return carry

    lax.fori_loop(1, total_devices, take_stat, 0)

    def total_of(i, carry):
        return carry[0] + stats[2 * i], carry[1] + stats[2 * i + 1]

    zero = jnp.zeros((PARTS, width), jnp.float32)
    even, odd = lax.fori_loop(0, total_devices // 2, total_of, (zero, zero))
    totals_ref[0] = even
    totals_ref[1] = odd

    for mk, cond in sent:
        when(cond, lambda: mk().wait_send())

    def done_stat(d, carry):
        stat(d).wait_send()
        return carry

    lax.fori_loop(1, total_devices, done_stat, 0)


def fused(blocks, owners, places, panel_matrix):
    R = lax.axis_size("row")
    C = lax.axis_size("col")
    S, BS, _ = blocks.shape
    CB, slab_rows, PW = panel_matrix.shape
    RB = CB * C // R
    width = PW // 2 // PARTS
    group = 2 * CB
    n_a = 12 * group // 16
    quarter = RB // CHIPS
    table = slot_table(owners, places, CB, RB)
    dma = lambda n: pltpu.SemaphoreType.DMA((n,))
    f32, bf16 = jnp.float32, blocks.dtype
    cfg = (R, S, CB, RB, BS, width, n_a)
    squares, totals = pl.pallas_call(
        functools.partial(panel_kernel, cfg),
        out_shape=(
            jax.ShapeDtypeStruct((quarter // 2 * BS, PW), f32),
            jax.ShapeDtypeStruct((2, PARTS, width), f32),
        ),
        in_specs=[pl.BlockSpec(memory_space=pl.ANY)] * 3,
        out_specs=[pl.BlockSpec(memory_space=pltpu.VMEM)] * 2,
        scratch_shapes=[
            pltpu.VMEM((CHIPS, group, BS, width), bf16),
            pltpu.VMEM((CHIPS, group, BS, width), bf16),
            pltpu.VMEM((S, BS, BS), bf16),
            pltpu.VMEM((S, BS, BS), bf16),
            pltpu.SMEM((8, 128), jnp.int32),
            pltpu.SMEM((8, 128), jnp.int32),
            pltpu.VMEM((8, 128), jnp.int32),
            pltpu.VMEM((2 * S + 1, BS, width), f32),
            pltpu.VMEM((PARTS, quarter, BS, width), f32),
            pltpu.VMEM((3, quarter, BS, width), jnp.int16),
            pltpu.VMEM((3, quarter, BS, width), jnp.int16),
            pltpu.VMEM((3, quarter, BS, width), jnp.int16),
            pltpu.VMEM((3, quarter, BS, width), jnp.int16),
            pltpu.VMEM((PARTS * 3, quarter, width), f32),
            pltpu.VMEM((PARTS * 3, quarter, width), f32),
            pltpu.VMEM((PARTS, quarter // 2, BS, width), f32),
            pltpu.VMEM((PARTS, quarter // 2, BS, width), f32),
            pltpu.VMEM((PARTS, quarter // 2, BS, width), f32),
            pltpu.VMEM((R * C, PARTS, width), f32),
            dma(5), dma(4), dma(4),
            dma(PARTS * 2 * R), dma(PARTS * 2 * R), dma(PARTS * 2 * R), dma(PARTS * 2 * R),
            dma(PARTS * 2 * R), dma(PARTS * 2 * R), dma(PARTS * 2 * R), dma(PARTS * 2 * R),
            dma(PARTS * 2), dma(PARTS * 2), dma(PARTS * 2), dma(PARTS * 2),
            dma(PARTS * 3), dma(PARTS * 3), dma(PARTS * 3), dma(PARTS * 3), dma(PARTS), dma(PARTS), dma(R * C), dma(R * C),
        ],
        compiler_params=pltpu.CompilerParams(
            collective_id=0, has_side_effects=True, vmem_limit_bytes=60 << 20
        ),
        cost_estimate=pl.CostEstimate(
            flops=2 * S * BS * BS * PW, bytes_accessed=4 << 20, transcendentals=0
        ),
    )(blocks, table, panel_matrix)
    col_mean = totals.reshape(PW) / (CB * C * BS)
    return squares / (col_mean + epsilon)


def on_device(blocks, owners, places, panel_matrix):
    col_count = lax.axis_size("col")
    row_count = lax.axis_size("row")
    col_blocks = panel_matrix.shape[0]
    block_side = blocks.shape[1]
    panel_width = panel_matrix.shape[2]
    row_blocks = col_blocks * col_count // row_count
    capacity = row_blocks * col_blocks // col_count
    targets = jnp.arange(col_count, dtype=jnp.int32)
    onehot = (owners[:, None] == targets[None, :]).astype(jnp.int32)
    before = jnp.cumsum(onehot, axis=0) - onehot
    bucket_rank = jnp.sum(before * onehot, axis=1)
    slot_index = owners * capacity + bucket_rank
    received = col_count * capacity
    outgoing = (
        jnp.zeros((received, block_side, block_side), blocks.dtype).at[slot_index].set(blocks)
    )
    out_places = jnp.zeros((received,), jnp.int32).at[slot_index].set(places)
    outgoing = outgoing.reshape(col_count, capacity, block_side, block_side)
    out_places = out_places.reshape(col_count, capacity)
    arrived, arrived_places = (
        lax.all_to_all(outgoing, "col", split_axis=0, concat_axis=0, tiled=True),
        lax.all_to_all(out_places, "col", split_axis=0, concat_axis=0, tiled=True),
    )
    arrived = arrived.reshape(received, block_side, block_side)
    arrived_places = arrived_places.reshape(received)
    row_in = arrived_places // col_blocks
    col_in = arrived_places % col_blocks
    panel_full = lax.all_gather(panel_matrix, "row", axis=1, tiled=True)
    group_size = min(32, received)
    turn_count = received // group_size

    def add_group(partial_value, members):
        tile_group, group_rows, group_cols = members
        pieces = panel_full[group_cols]
        product = jnp.einsum("sab,sbp->sap", tile_group, pieces, preferred_element_type=jnp.float32)
        return (partial_value.at[group_rows].add(product), None)

    start_sum = jnp.zeros((row_blocks, block_side, panel_width), jnp.float32)
    partial_value = lax.scan(
        add_group,
        start_sum,
        (
            arrived.reshape(turn_count, group_size, block_side, block_side),
            row_in.reshape(turn_count, group_size),
            col_in.reshape(turn_count, group_size),
        ),
    )[0]
    partial_rows = partial_value.reshape(row_blocks * block_side, panel_width)
    own_rows = lax.psum_scatter(partial_rows, "col", scatter_dimension=0, tiled=True)
    squares = own_rows * own_rows
    totals = lax.psum(jnp.sum(squares, axis=0), ("row", "col"))
    col_mean = totals / (col_blocks * col_count * block_side)
    return squares / (col_mean + epsilon)


def solution(mesh):
    fits = mesh.shape["col"] == 2 * CHIPS and mesh.shape["row"] == 4
    placed = (
        P(("row", "col"), None, None),
        P(("row", "col")),
        P(("row", "col")),
        P("col", "row", None),
    )
    return jax.shard_map(
        fused if fits else on_device, mesh=mesh, in_specs=placed, out_specs=P(("row", "col"), None), check_vma=False
    )
```

```python
import functools

import jax
import jax.numpy as jnp
from jax import lax
from jax.experimental import pallas as pl
from jax.experimental.pallas import tpu as pltpu
from jax.sharding import PartitionSpec as P

epsilon = 1e-06
CHIPS = 4
PARTS = 2
UNROLL = 8
LEVELS = 32767.0
smallest = 1e-30
MESH = pl.DeviceIdType.MESH


def slot_table(owners, places, col_blocks, row_blocks):
    count = owners.shape[0]
    ids = jnp.arange(count, dtype=jnp.int32)
    rows = places // col_blocks
    cols = owners * col_blocks + places % col_blocks
    targets = jnp.arange(row_blocks, dtype=jnp.int32)
    member = (rows[None, :] == targets[:, None]).astype(jnp.int32)
    held = jnp.sum(member, axis=1)
    filled = held + held % 2
    below = (targets[None, :] < targets[:, None]).astype(jnp.int32)
    base = jnp.sum(below * filled[None, :], axis=1)
    earlier = jnp.logical_and(rows[None, :] == rows[:, None], ids[None, :] < ids[:, None])
    rank = jnp.sum(earlier.astype(jnp.int32), axis=1)
    at = rank + jnp.sum(member * base[:, None], axis=0)
    entries = jnp.arange(count + row_blocks, dtype=jnp.int32)
    chosen = (at[None, :] == entries[:, None]).astype(jnp.int32)
    code = jnp.sum(chosen * (cols * 2 * count + ids - count)[None, :], axis=1) + count
    pairs = entries[: entries.shape[0] // 2]
    starts = jnp.logical_and(base[None, :] == 2 * pairs[:, None], held[None, :] > 0)
    first = jnp.any(starts, axis=1).astype(jnp.int32)
    last = jnp.where(held > 0, (base + filled) // 2, 0)
    lines = [jnp.pad(v, (0, 128 - v.shape[0])) for v in (code, first, last)]
    return jnp.stack(lines + [jnp.zeros((128,), jnp.int32)] * 5)


def panel_kernel(
    cfg,
    blocks_ref, table_ref, panel_ref,
    squares_ref, totals_ref,
    pan0, pan1, own_blocks, sib_blocks, own_table, sib_table, sib_table_vmem,
    run, part, code0, code1, arrive0, arrive1, scale_out, scale_in, sib_in, sib_out, mine, stats,
    local_sem, pair_send, pair_recv,
    za_send, za_recv, zb_send, zb_recv,
    xa_send, xa_recv, ra_send, ra_recv,
    xb_send, xb_recv, rb_send, rb_recv,
    rs_send, rs_recv, sc_send, sc_recv, out_send, out_recv, st_send, st_recv,
):
    R, S, CB, RB, BS, width, n_a = cfg
    C = 2 * CHIPS
    slab_rows = BS // R
    group = 2 * CB
    pairs = (S + RB) // 2
    quarter = RB // CHIPS
    own_rows = quarter // 2
    pans, codes, arrives = (pan0, pan1), (code0, code1), (arrive0, arrive1)
    z = lax.axis_index("row")
    c = lax.axis_index("col")
    q = c // 2
    k = c % 2
    qx = q + 1 - 2 * (q % 2)
    qy = lax.rem(q + 2, 4)
    qd = 3 - q
    me = z * C + c
    total_devices = R * C
    nbrs = (qx, qy)
    sent = []

    def true():
        return None

    def when(cond, f):
        if cond is None:
            f()
        else:
            pl.when(cond)(f)

    def start(mk, cond=None):
        when(cond, lambda: mk().start())
        sent.append((mk, cond))

    def remote(src, dst, s, r, dev):
        return pltpu.make_async_remote_copy(
            src_ref=src, dst_ref=dst, send_sem=s, recv_sem=r, device_id=dev, device_id_type=MESH
        )

    barrier = pltpu.get_barrier_semaphore()

    def greet(d, carry):
        t = lax.rem(me + d, total_devices)
        pl.semaphore_signal(barrier, inc=1, device_id=(t // C, t % C), device_id_type=MESH)
        return carry

    lax.fori_loop(1, total_devices, greet, 0)

    def slab(zz):
        return pl.ds(pl.multiple_of(zz * slab_rows, slab_rows), slab_rows)

    def local(i, src, dst):
        return pltpu.make_async_copy(src, dst, local_sem.at[i])

    def panel_cols(core, j):
        return pl.ds(pl.multiple_of((core * PARTS + j) * width, width), width)

    for j in range(PARTS):
        local(
            j, panel_ref.at[:, :, panel_cols(k, j)],
            pans[j].at[q, pl.ds(k * CB, CB), slab(z)],
        ).start()
    local(2, table_ref, own_table).start()
    local(3, blocks_ref, own_blocks.at[pl.ds(0, S)]).start()
    pl.semaphore_wait(barrier, total_devices - 1)

    sib = (z, q * 2 + 1 - k)

    def pair_panel(j):
        return remote(
            panel_ref.at[:, :, panel_cols(1 - k, j)],
            pans[j].at[q, pl.ds(k * CB, CB), slab(z)],
            pair_send.at[j], pair_recv.at[j], sib,
        )

    for j in range(PARTS):
        start(functools.partial(pair_panel, j))

    def pair_table():
        return remote(table_ref, sib_table_vmem, pair_send.at[2], pair_recv.at[2], sib)

    def pair_blocks():
        return remote(blocks_ref, sib_blocks.at[pl.ds(0, S)], pair_send.at[3], pair_recv.at[3], sib)

    start(pair_table)
    start(pair_blocks)

    def dev_q(qq):
        return (z, qq * 2 + k)

    def a_range(part):
        half = n_a // 2
        return (pl.ds(0, n_a), pl.ds(0, half), pl.ds(half, n_a - half))[part]

    def b_range(part):
        n_b = group - n_a
        half = n_b // 2
        return (pl.ds(n_a, n_b), pl.ds(n_a, half), pl.ds(n_a + half, n_b - half))[part]

    def za(j, up, d):
        shard = z - (d - 1) if up else z + (d - 1)
        view = pans[j].at[q, a_range(0), slab(jnp.clip(shard, 0, R - 1))]
        i = (j * 2 + up) * R + d - 1
        to = jnp.clip(z + 1 if up else z - 1, 0, R - 1)
        return remote(view, view, za_send.at[i], za_recv.at[i], (to, c))

    def zb(j, up, d):
        shard = z - (d - 1) if up else z + (d - 1)
        view = pans[j].at[:, b_range(0), slab(jnp.clip(shard, 0, R - 1))]
        i = (j * 2 + up) * R + d - 1
        to = jnp.clip(z + 1 if up else z - 1, 0, R - 1)
        return remote(view, view, zb_send.at[i], zb_recv.at[i], (to, c))

    def z_send_cond(up, d):
        if up:
            return jnp.logical_and(z - (d - 1) >= 0, z + 1 < R)
        return jnp.logical_and(z + (d - 1) < R, z - 1 >= 0)

    def z_recv_cond(up, d):
        return z - d >= 0 if up else z + d < R

    def z_from(up, d):
        return jnp.clip(z - d if up else z + d, 0, R - 1)

    def xa(j, n, zz):
        view = pans[j].at[q, a_range(0), slab(zz)]
        i = (j * 2 + n) * R + zz
        return remote(view, view, xa_send.at[i], xa_recv.at[i], dev_q(nbrs[n]))

    def ra(j, n, zz):
        view = pans[j].at[nbrs[n], a_range(1 + n), slab(zz)]
        i = (j * 2 + n) * R + zz
        return remote(view, view, ra_send.at[i], ra_recv.at[i], dev_q(nbrs[1 - n]))

    def xb(j, n):
        view = pans[j].at[q, b_range(0), slab(z)]
        i = j * 2 + n
        return remote(view, view, xb_send.at[i], xb_recv.at[i], dev_q(nbrs[n]))

    def rb(j, n):
        view = pans[j].at[nbrs[n], b_range(1 + n), slab(z)]
        i = j * 2 + n
        return remote(view, view, rb_send.at[i], rb_recv.at[i], dev_q(nbrs[1 - n]))

    p = functools.partial

    def gather_step(j, s):
        if s == 0:
            local(
                j, panel_ref.at[:, :, panel_cols(k, j)],
                pans[j].at[q, pl.ds(k * CB, CB), slab(z)],
            ).wait()
            pair_panel(j).wait_recv()
            for up in (1, 0):
                start(p(za, j, up, 1), z_send_cond(up, 1))
            for n in (0, 1):
                start(p(xb, j, n))
            for n in (0, 1):
                start(p(xa, j, n, z))
            return
        if s == 1:
            for n in (0, 1):
                xb(j, n).wait_recv()
                start(p(rb, j, n))
        if s == 2:
            for n in (0, 1):
                rb(j, n).wait_recv()
            for up in (1, 0):
                start(p(zb, j, up, 1), z_send_cond(up, 1))
        if s < R:
            for up in (1, 0):
                cond = z_recv_cond(up, s)
                when(cond, lambda: za(j, up, s).wait_recv())
                if s < R - 1:
                    start(p(za, j, up, s + 1), z_send_cond(up, s + 1))
                for n in (0, 1):
                    start(p(xa, j, n, z_from(up, s)), cond)
        if 1 <= s <= R:
            d = s - 1
            for up in (1, 0) if d else (1,):
                cond = z_recv_cond(up, d) if d else None
                zz = z_from(up, d)
                for n in (0, 1):
                    when(cond, lambda: xa(j, n, zz).wait_recv())
                    start(p(ra, j, n, zz), cond)
        if s >= 3:
            d = s - 2
            for up in (1, 0):
                when(z_recv_cond(up, d), lambda: zb(j, up, d).wait_recv())
                if d < R - 1:
                    start(p(zb, j, up, d + 1), z_send_cond(up, d + 1))
        if s == steps - 1:
            for zz in range(R):
                for n in (0, 1):
                    ra(j, n, zz).wait_recv()

    steps = R + 2

    def multiply(j, blocks, table, base):
        pan = pans[j]

        def turn(g, acc):
            for u in range(UNROLL):
                t = g * UNROLL + u
                tiles, pieces = [], []
                for e in (0, 1):
                    code = table[0, 2 * t + e]
                    col = lax.div(code, 2 * S)
                    tiles.append(blocks[lax.rem(code, 2 * S)])
                    pieces.append(pan[lax.div(col, group), lax.rem(col, group)])
                product = jnp.dot(
                    jnp.concatenate(tiles, axis=1), jnp.concatenate(pieces, axis=0),
                    preferred_element_type=jnp.float32,
                )
                acc = jnp.where(table[1, t] == 1, 0.0, acc) + product
                run[base + t] = acc
            return acc

        lax.fori_loop(0, pairs // UNROLL, turn, jnp.zeros((BS, width), jnp.float32))

    others = (qx, qy, qd)

    def scatter(j, rel):
        i = j * 3 + rel
        return remote(
            codes[j].at[rel], arrives[j].at[rel], rs_send.at[i], rs_recv.at[i],
            dev_q(others[rel]),
        )

    def scatter_scale(j, rel):
        i = j * 3 + rel
        return remote(
            scale_out.at[i], scale_in.at[i], sc_send.at[i], sc_recv.at[i], dev_q(others[rel])
        )

    def row_sum(i):
        a = own_table[2, i]
        b = sib_table[2, i]
        b = jnp.where(b > 0, b + pairs, 0)
        return run[a] + run[b]

    def add_rows(j):
        for rel in (2, 0, 1):
            for b in range(quarter):
                value = row_sum(others[rel] * quarter + b)
                top = jnp.max(jnp.abs(value), axis=0, keepdims=True)
                top = jnp.maximum(top, smallest)
                codes[j][rel, b] = jnp.round(value * (LEVELS / top)).astype(jnp.int32).astype(jnp.int16)
                scale_out[j * 3 + rel, pl.ds(b, 1)] = top * (1.0 / LEVELS)
            start(p(scatter_scale, j, rel))
            start(p(scatter, j, rel))
        for b in range(quarter):
            part[j, b] = row_sum(q * quarter + b)

    def pair_rows(j):
        return remote(sib_out.at[j], sib_in.at[j], out_send.at[j], out_recv.at[j], sib)

    def square(j):
        for rel in range(3):
            scatter_scale(j, rel).wait_recv()
            scatter(j, rel).wait_recv()

        def block(b, total, keep):
            value = part[j, b]
            for rel in range(3):
                code = arrives[j][rel, b].astype(jnp.int32).astype(jnp.float32)
                value = value + code * scale_in[j * 3 + rel, pl.ds(b, 1)]
            value = value * value
            keep(value)
            return total + jnp.sum(value.reshape(BS // 8, 8, width), axis=0)

        total = jnp.zeros((8, width), jnp.float32)
        for i in range(own_rows):
            def keep(value):
                sib_out[j, i] = value
            total = block((1 - k) * own_rows + i, total, keep)
        start(p(pair_rows, j))
        for i in range(own_rows):
            def keep_mine(value):
                mine[j, i] = value
            total = block(k * own_rows + i, total, keep_mine)
        stats[me, pl.ds(j, 1)] = jnp.sum(total, axis=0, keepdims=True)

    lag = 2
    for s in range(steps):
        gather_step(0, s)
        if s >= lag:
            gather_step(1, s - lag)
    local(2, table_ref, own_table).wait()
    local(3, blocks_ref, own_blocks.at[pl.ds(0, S)]).wait()
    pair_table().wait_recv()
    local(4, sib_table_vmem, sib_table).start()
    run[0] = jnp.zeros((BS, width), jnp.float32)
    for held in (own_blocks, sib_blocks):
        held[S] = jnp.zeros((BS, BS), held.dtype)
    local(4, sib_table_vmem, sib_table).wait()
    pair_blocks().wait_recv()
    multiply(0, own_blocks, own_table, 1)
    gather_step(1, steps - 2)
    multiply(0, sib_blocks, sib_table, 1 + pairs)
    add_rows(0)
    gather_step(1, steps - 1)
    multiply(1, own_blocks, own_table, 1)
    multiply(1, sib_blocks, sib_table, 1 + pairs)
    add_rows(1)
    square(0)
    square(1)

    def stat(d):
        t = lax.rem(me + d, total_devices)
        return remote(
            stats.at[me], stats.at[me], st_send.at[t], st_recv.at[me], (t // C, t % C)
        )

    def stat_from(d):
        t = lax.rem(me + d, total_devices)
        return remote(
            stats.at[t], stats.at[t], st_send.at[t], st_recv.at[t], (t // C, t % C)
        )

    def send_stat(d, carry):
        stat(d).start()
        return carry

    lax.fori_loop(1, total_devices, send_stat, 0)

    def put(j, core, value_of):
        for i in range(own_rows):
            squares_ref[pl.ds(i * BS, BS), panel_cols(core, j)] = value_of(i)

    for j in range(PARTS):
        put(j, k, lambda i: mine[j, i])
    for j in range(PARTS):
        pair_rows(j).wait_recv()
        put(j, 1 - k, lambda i: sib_in[j, i])

    def take_stat(d, carry):
        stat_from(d).wait_recv()
        return carry

    lax.fori_loop(1, total_devices, take_stat, 0)

    def total_of(i, carry):
        return carry[0] + stats[2 * i], carry[1] + stats[2 * i + 1]

    zero = jnp.zeros((PARTS, width), jnp.float32)
    even, odd = lax.fori_loop(0, total_devices // 2, total_of, (zero, zero))
    totals_ref[0] = even
    totals_ref[1] = odd

    for mk, cond in sent:
        when(cond, lambda: mk().wait_send())

    def done_stat(d, carry):
        stat(d).wait_send()
        return carry

    lax.fori_loop(1, total_devices, done_stat, 0)


def fused(blocks, owners, places, panel_matrix):
    R = lax.axis_size("row")
    C = lax.axis_size("col")
    S, BS, _ = blocks.shape
    CB, slab_rows, PW = panel_matrix.shape
    RB = CB * C // R
    width = PW // 2 // PARTS
    group = 2 * CB
    n_a = 12 * group // 16
    quarter = RB // CHIPS
    table = slot_table(owners, places, CB, RB)
    dma = lambda n: pltpu.SemaphoreType.DMA((n,))
    f32, bf16 = jnp.float32, blocks.dtype
    cfg = (R, S, CB, RB, BS, width, n_a)
    squares, totals = pl.pallas_call(
        functools.partial(panel_kernel, cfg),
        out_shape=(
            jax.ShapeDtypeStruct((quarter // 2 * BS, PW), f32),
            jax.ShapeDtypeStruct((2, PARTS, width), f32),
        ),
        in_specs=[pl.BlockSpec(memory_space=pl.ANY)] * 3,
        out_specs=[pl.BlockSpec(memory_space=pltpu.VMEM)] * 2,
        scratch_shapes=[
            pltpu.VMEM((CHIPS, group, BS, width), bf16),
            pltpu.VMEM((CHIPS, group, BS, width), bf16),
            pltpu.VMEM((S + 1, BS, BS), bf16),
            pltpu.VMEM((S + 1, BS, BS), bf16),
            pltpu.SMEM((8, 128), jnp.int32),
            pltpu.SMEM((8, 128), jnp.int32),
            pltpu.VMEM((8, 128), jnp.int32),
            pltpu.VMEM((S + RB + 1, BS, width), f32),
            pltpu.VMEM((PARTS, quarter, BS, width), f32),
            pltpu.VMEM((3, quarter, BS, width), jnp.int16),
            pltpu.VMEM((3, quarter, BS, width), jnp.int16),
            pltpu.VMEM((3, quarter, BS, width), jnp.int16),
            pltpu.VMEM((3, quarter, BS, width), jnp.int16),
            pltpu.VMEM((PARTS * 3, quarter, width), f32),
            pltpu.VMEM((PARTS * 3, quarter, width), f32),
            pltpu.VMEM((PARTS, quarter // 2, BS, width), f32),
            pltpu.VMEM((PARTS, quarter // 2, BS, width), f32),
            pltpu.VMEM((PARTS, quarter // 2, BS, width), f32),
            pltpu.VMEM((R * C, PARTS, width), f32),
            dma(5), dma(4), dma(4),
            dma(PARTS * 2 * R), dma(PARTS * 2 * R), dma(PARTS * 2 * R), dma(PARTS * 2 * R),
            dma(PARTS * 2 * R), dma(PARTS * 2 * R), dma(PARTS * 2 * R), dma(PARTS * 2 * R),
            dma(PARTS * 2), dma(PARTS * 2), dma(PARTS * 2), dma(PARTS * 2),
            dma(PARTS * 3), dma(PARTS * 3), dma(PARTS * 3), dma(PARTS * 3), dma(PARTS), dma(PARTS), dma(R * C), dma(R * C),
        ],
        compiler_params=pltpu.CompilerParams(
            collective_id=0, has_side_effects=True, vmem_limit_bytes=60 << 20
        ),
        cost_estimate=pl.CostEstimate(
            flops=2 * S * BS * BS * PW, bytes_accessed=4 << 20, transcendentals=0
        ),
    )(blocks, table, panel_matrix)
    col_mean = totals.reshape(PW) / (CB * C * BS)
    return squares / (col_mean + epsilon)


def on_device(blocks, owners, places, panel_matrix):
    col_count = lax.axis_size("col")
    row_count = lax.axis_size("row")
    col_blocks = panel_matrix.shape[0]
    block_side = blocks.shape[1]
    panel_width = panel_matrix.shape[2]
    row_blocks = col_blocks * col_count // row_count
    capacity = row_blocks * col_blocks // col_count
    targets = jnp.arange(col_count, dtype=jnp.int32)
    onehot = (owners[:, None] == targets[None, :]).astype(jnp.int32)
    before = jnp.cumsum(onehot, axis=0) - onehot
    bucket_rank = jnp.sum(before * onehot, axis=1)
    slot_index = owners * capacity + bucket_rank
    received = col_count * capacity
    outgoing = (
        jnp.zeros((received, block_side, block_side), blocks.dtype).at[slot_index].set(blocks)
    )
    out_places = jnp.zeros((received,), jnp.int32).at[slot_index].set(places)
    outgoing = outgoing.reshape(col_count, capacity, block_side, block_side)
    out_places = out_places.reshape(col_count, capacity)
    arrived, arrived_places = (
        lax.all_to_all(outgoing, "col", split_axis=0, concat_axis=0, tiled=True),
        lax.all_to_all(out_places, "col", split_axis=0, concat_axis=0, tiled=True),
    )
    arrived = arrived.reshape(received, block_side, block_side)
    arrived_places = arrived_places.reshape(received)
    row_in = arrived_places // col_blocks
    col_in = arrived_places % col_blocks
    panel_full = lax.all_gather(panel_matrix, "row", axis=1, tiled=True)
    group_size = min(32, received)
    turn_count = received // group_size

    def add_group(partial_value, members):
        tile_group, group_rows, group_cols = members
        pieces = panel_full[group_cols]
        product = jnp.einsum("sab,sbp->sap", tile_group, pieces, preferred_element_type=jnp.float32)
        return (partial_value.at[group_rows].add(product), None)

    start_sum = jnp.zeros((row_blocks, block_side, panel_width), jnp.float32)
    partial_value = lax.scan(
        add_group,
        start_sum,
        (
            arrived.reshape(turn_count, group_size, block_side, block_side),
            row_in.reshape(turn_count, group_size),
            col_in.reshape(turn_count, group_size),
        ),
    )[0]
    partial_rows = partial_value.reshape(row_blocks * block_side, panel_width)
    own_rows = lax.psum_scatter(partial_rows, "col", scatter_dimension=0, tiled=True)
    squares = own_rows * own_rows
    totals = lax.psum(jnp.sum(squares, axis=0), ("row", "col"))
    col_mean = totals / (col_blocks * col_count * block_side)
    return squares / (col_mean + epsilon)


def solution(mesh):
    fits = mesh.shape["col"] == 2 * CHIPS and mesh.shape["row"] == 4
    placed = (
        P(("row", "col"), None, None),
        P(("row", "col")),
        P(("row", "col")),
        P("col", "row", None),
    )
    return jax.shard_map(
        fused if fits else on_device, mesh=mesh, in_specs=placed, out_specs=P(("row", "col"), None), check_vma=False
    )
```

```python
import functools

import jax
import jax.numpy as jnp
from jax import lax
from jax.experimental import pallas as pl
from jax.experimental.pallas import tpu as pltpu
from jax.sharding import PartitionSpec as P

epsilon = 1e-06
CHIPS = 4
PARTS = 2
UNROLL = 8
LEVELS = 32767.0
smallest = 1e-30
MESH = pl.DeviceIdType.MESH


def slot_table(owners, places, col_blocks, row_blocks):
    count = owners.shape[0]
    ids = jnp.arange(count, dtype=jnp.int32)
    rows = places // col_blocks
    cols = owners * col_blocks + places % col_blocks
    targets = jnp.arange(row_blocks, dtype=jnp.int32)
    member = (rows[None, :] == targets[:, None]).astype(jnp.int32)
    held = jnp.sum(member, axis=1)
    filled = held + held % 2
    below = (targets[None, :] < targets[:, None]).astype(jnp.int32)
    base = jnp.sum(below * filled[None, :], axis=1)
    earlier = jnp.logical_and(rows[None, :] == rows[:, None], ids[None, :] < ids[:, None])
    rank = jnp.sum(earlier.astype(jnp.int32), axis=1)
    at = rank + jnp.sum(member * base[:, None], axis=0)
    entries = jnp.arange(count + row_blocks, dtype=jnp.int32)
    chosen = (at[None, :] == entries[:, None]).astype(jnp.int32)
    code = jnp.sum(chosen * (cols * 2 * count + ids - count)[None, :], axis=1) + count
    pairs = entries[: entries.shape[0] // 2]
    starts = jnp.logical_and(base[None, :] == 2 * pairs[:, None], held[None, :] > 0)
    first = jnp.any(starts, axis=1).astype(jnp.int32)
    last = jnp.where(held > 0, (base + filled) // 2, 0)
    lines = [jnp.pad(v, (0, 128 - v.shape[0])) for v in (code, first, last)]
    return jnp.stack(lines + [jnp.zeros((128,), jnp.int32)] * 5)


def panel_kernel(
    cfg,
    blocks_ref, table_ref, panel_ref,
    squares_ref, totals_ref,
    pan0, pan1, own_blocks, sib_blocks, own_table, sib_table, sib_table_vmem,
    run, part, code0, code1, arrive0, arrive1, scale_out, scale_in, sib_in, sib_out, mine, stats,
    local_sem, pair_send, pair_recv,
    za_send, za_recv, zb_send, zb_recv,
    xa_send, xa_recv, ra_send, ra_recv,
    xb_send, xb_recv, rb_send, rb_recv,
    rs_send, rs_recv, sc_send, sc_recv, out_send, out_recv, st_send, st_recv,
):
    R, S, CB, RB, BS, width, n_a = cfg
    C = 2 * CHIPS
    slab_rows = BS // R
    group = 2 * CB
    pairs = (S + RB) // 2
    quarter = RB // CHIPS
    own_rows = quarter // 2
    pans, codes, arrives = (pan0, pan1), (code0, code1), (arrive0, arrive1)
    z = lax.axis_index("row")
    c = lax.axis_index("col")
    q = c // 2
    k = c % 2
    qx = q + 1 - 2 * (q % 2)
    qy = lax.rem(q + 2, 4)
    qd = 3 - q
    me = z * C + c
    total_devices = R * C
    nbrs = (qx, qy)
    sent = []

    def true():
        return None

    def when(cond, f):
        if cond is None:
            f()
        else:
            pl.when(cond)(f)

    def start(mk, cond=None):
        when(cond, lambda: mk().start())
        sent.append((mk, cond))

    def remote(src, dst, s, r, dev):
        return pltpu.make_async_remote_copy(
            src_ref=src, dst_ref=dst, send_sem=s, recv_sem=r, device_id=dev, device_id_type=MESH
        )

    barrier = pltpu.get_barrier_semaphore()

    def greet(d, carry):
        t = lax.rem(me + d, total_devices)
        pl.semaphore_signal(barrier, inc=1, device_id=(t // C, t % C), device_id_type=MESH)
        return carry

    lax.fori_loop(1, total_devices, greet, 0)

    def slab(zz):
        return pl.ds(pl.multiple_of(zz * slab_rows, slab_rows), slab_rows)

    def local(i, src, dst):
        return pltpu.make_async_copy(src, dst, local_sem.at[i])

    def panel_cols(core, j):
        return pl.ds(pl.multiple_of((core * PARTS + j) * width, width), width)

    for j in range(PARTS):
        local(
            j, panel_ref.at[:, :, panel_cols(k, j)],
            pans[j].at[q, pl.ds(k * CB, CB), slab(z)],
        ).start()
    local(2, table_ref, own_table).start()
    pl.semaphore_wait(barrier, total_devices - 1)

    sib = (z, q * 2 + 1 - k)

    def pair_panel(j):
        return remote(
            panel_ref.at[:, :, panel_cols(1 - k, j)],
            pans[j].at[q, pl.ds(k * CB, CB), slab(z)],
            pair_send.at[j], pair_recv.at[j], sib,
        )

    for j in range(PARTS):
        start(functools.partial(pair_panel, j))

    def pair_table():
        return remote(table_ref, sib_table_vmem, pair_send.at[2], pair_recv.at[2], sib)

    def pair_blocks():
        return remote(blocks_ref, sib_blocks.at[pl.ds(0, S)], pair_send.at[3], pair_recv.at[3], sib)

    start(pair_table)

    def dev_q(qq):
        return (z, qq * 2 + k)

    def a_range(part):
        half = n_a // 2
        return (pl.ds(0, n_a), pl.ds(0, half), pl.ds(half, n_a - half))[part]

    def b_range(part):
        n_b = group - n_a
        half = n_b // 2
        return (pl.ds(n_a, n_b), pl.ds(n_a, half), pl.ds(n_a + half, n_b - half))[part]

    def za(j, up, d):
        shard = z - (d - 1) if up else z + (d - 1)
        view = pans[j].at[q, a_range(0), slab(jnp.clip(shard, 0, R - 1))]
        i = (j * 2 + up) * R + d - 1
        to = jnp.clip(z + 1 if up else z - 1, 0, R - 1)
        return remote(view, view, za_send.at[i], za_recv.at[i], (to, c))

    def zb(j, up, d):
        shard = z - (d - 1) if up else z + (d - 1)
        view = pans[j].at[:, b_range(0), slab(jnp.clip(shard, 0, R - 1))]
        i = (j * 2 + up) * R + d - 1
        to = jnp.clip(z + 1 if up else z - 1, 0, R - 1)
        return remote(view, view, zb_send.at[i], zb_recv.at[i], (to, c))

    def z_send_cond(up, d):
        if up:
            return jnp.logical_and(z - (d - 1) >= 0, z + 1 < R)
        return jnp.logical_and(z + (d - 1) < R, z - 1 >= 0)

    def z_recv_cond(up, d):
        return z - d >= 0 if up else z + d < R

    def z_from(up, d):
        return jnp.clip(z - d if up else z + d, 0, R - 1)

    def xa(j, n, zz):
        view = pans[j].at[q, a_range(0), slab(zz)]
        i = (j * 2 + n) * R + zz
        return remote(view, view, xa_send.at[i], xa_recv.at[i], dev_q(nbrs[n]))

    def ra(j, n, zz):
        view = pans[j].at[nbrs[n], a_range(1 + n), slab(zz)]
        i = (j * 2 + n) * R + zz
        return remote(view, view, ra_send.at[i], ra_recv.at[i], dev_q(nbrs[1 - n]))

    def xb(j, n):
        view = pans[j].at[q, b_range(0), slab(z)]
        i = j * 2 + n
        return remote(view, view, xb_send.at[i], xb_recv.at[i], dev_q(nbrs[n]))

    def rb(j, n):
        view = pans[j].at[nbrs[n], b_range(1 + n), slab(z)]
        i = j * 2 + n
        return remote(view, view, rb_send.at[i], rb_recv.at[i], dev_q(nbrs[1 - n]))

    p = functools.partial

    def gather_step(j, s):
        if s == 0:
            local(
                j, panel_ref.at[:, :, panel_cols(k, j)],
                pans[j].at[q, pl.ds(k * CB, CB), slab(z)],
            ).wait()
            pair_panel(j).wait_recv()
            for up in (1, 0):
                start(p(za, j, up, 1), z_send_cond(up, 1))
            for n in (0, 1):
                start(p(xb, j, n))
            for n in (0, 1):
                start(p(xa, j, n, z))
            return
        if s == 1:
            for n in (0, 1):
                xb(j, n).wait_recv()
                start(p(rb, j, n))
        if s == 2:
            for n in (0, 1):
                rb(j, n).wait_recv()
            for up in (1, 0):
                start(p(zb, j, up, 1), z_send_cond(up, 1))
        if s < R:
            for up in (1, 0):
                cond = z_recv_cond(up, s)
                when(cond, lambda: za(j, up, s).wait_recv())
                if s < R - 1:
                    start(p(za, j, up, s + 1), z_send_cond(up, s + 1))
                for n in (0, 1):
                    start(p(xa, j, n, z_from(up, s)), cond)
        if 1 <= s <= R:
            d = s - 1
            for up in (1, 0) if d else (1,):
                cond = z_recv_cond(up, d) if d else None
                zz = z_from(up, d)
                for n in (0, 1):
                    when(cond, lambda: xa(j, n, zz).wait_recv())
                    start(p(ra, j, n, zz), cond)
        if s >= 3:
            d = s - 2
            for up in (1, 0):
                when(z_recv_cond(up, d), lambda: zb(j, up, d).wait_recv())
                if d < R - 1:
                    start(p(zb, j, up, d + 1), z_send_cond(up, d + 1))
        if s == steps - 1:
            for zz in range(R):
                for n in (0, 1):
                    ra(j, n, zz).wait_recv()

    steps = R + 2

    def multiply(j, blocks, table, base):
        pan = pans[j]

        def turn(g, acc):
            for u in range(UNROLL):
                t = g * UNROLL + u
                tiles, pieces = [], []
                for e in (0, 1):
                    code = table[0, 2 * t + e]
                    col = lax.div(code, 2 * S)
                    tiles.append(blocks[lax.rem(code, 2 * S)])
                    pieces.append(pan[lax.div(col, group), lax.rem(col, group)])
                product = jnp.dot(
                    jnp.concatenate(tiles, axis=1), jnp.concatenate(pieces, axis=0),
                    preferred_element_type=jnp.float32,
                )
                acc = jnp.where(table[1, t] == 1, 0.0, acc) + product
                run[base + t] = acc
            return acc

        lax.fori_loop(0, pairs // UNROLL, turn, jnp.zeros((BS, width), jnp.float32))

    others = (qx, qy, qd)

    def scatter(j, rel):
        i = j * 3 + rel
        return remote(
            codes[j].at[rel], arrives[j].at[rel], rs_send.at[i], rs_recv.at[i],
            dev_q(others[rel]),
        )

    def scatter_scale(j, rel):
        i = j * 3 + rel
        return remote(
            scale_out.at[i], scale_in.at[i], sc_send.at[i], sc_recv.at[i], dev_q(others[rel])
        )

    def row_sum(i):
        a = own_table[2, i]
        b = sib_table[2, i]
        b = jnp.where(b > 0, b + pairs, 0)
        return run[a] + run[b]

    def add_rows(j):
        for rel in (2, 0, 1):
            for b in range(quarter):
                value = row_sum(others[rel] * quarter + b)
                top = jnp.max(jnp.abs(value), axis=0, keepdims=True)
                top = jnp.maximum(top, smallest)
                codes[j][rel, b] = jnp.round(value * (LEVELS / top)).astype(jnp.int32).astype(jnp.int16)
                scale_out[j * 3 + rel, pl.ds(b, 1)] = top * (1.0 / LEVELS)
            start(p(scatter_scale, j, rel))
            start(p(scatter, j, rel))
        for b in range(quarter):
            part[j, b] = row_sum(q * quarter + b)

    def pair_rows(j):
        return remote(sib_out.at[j], sib_in.at[j], out_send.at[j], out_recv.at[j], sib)

    def square(j):
        for rel in range(3):
            scatter_scale(j, rel).wait_recv()
            scatter(j, rel).wait_recv()

        def block(b, total, keep):
            value = part[j, b]
            for rel in range(3):
                code = arrives[j][rel, b].astype(jnp.int32).astype(jnp.float32)
                value = value + code * scale_in[j * 3 + rel, pl.ds(b, 1)]
            value = value * value
            keep(value)
            return total + jnp.sum(value.reshape(BS // 8, 8, width), axis=0)

        total = jnp.zeros((8, width), jnp.float32)
        for i in range(own_rows):
            def keep(value):
                sib_out[j, i] = value
            total = block((1 - k) * own_rows + i, total, keep)
        start(p(pair_rows, j))
        for i in range(own_rows):
            def keep_mine(value):
                mine[j, i] = value
            total = block(k * own_rows + i, total, keep_mine)
        stats[me, pl.ds(j, 1)] = jnp.sum(total, axis=0, keepdims=True)

    lag = 2
    for s in range(steps):
        gather_step(0, s)
        if s >= lag:
            gather_step(1, s - lag)
        if s == lag:
            start(pair_blocks)
            local(3, blocks_ref, own_blocks.at[pl.ds(0, S)]).start()
    local(2, table_ref, own_table).wait()
    local(3, blocks_ref, own_blocks.at[pl.ds(0, S)]).wait()
    pair_table().wait_recv()
    local(4, sib_table_vmem, sib_table).start()
    run[0] = jnp.zeros((BS, width), jnp.float32)
    for held in (own_blocks, sib_blocks):
        held[S] = jnp.zeros((BS, BS), held.dtype)
    local(4, sib_table_vmem, sib_table).wait()
    pair_blocks().wait_recv()
    multiply(0, own_blocks, own_table, 1)
    gather_step(1, steps - 2)
    multiply(0, sib_blocks, sib_table, 1 + pairs)
    add_rows(0)
    gather_step(1, steps - 1)
    multiply(1, own_blocks, own_table, 1)
    multiply(1, sib_blocks, sib_table, 1 + pairs)
    add_rows(1)
    square(0)
    square(1)

    def stat(d):
        t = lax.rem(me + d, total_devices)
        return remote(
            stats.at[me], stats.at[me], st_send.at[t], st_recv.at[me], (t // C, t % C)
        )

    def stat_from(d):
        t = lax.rem(me + d, total_devices)
        return remote(
            stats.at[t], stats.at[t], st_send.at[t], st_recv.at[t], (t // C, t % C)
        )

    def send_stat(d, carry):
        stat(d).start()
        return carry

    lax.fori_loop(1, total_devices, send_stat, 0)

    def put(j, core, value_of):
        for i in range(own_rows):
            squares_ref[pl.ds(i * BS, BS), panel_cols(core, j)] = value_of(i)

    for j in range(PARTS):
        put(j, k, lambda i: mine[j, i])
    for j in range(PARTS):
        pair_rows(j).wait_recv()
        put(j, 1 - k, lambda i: sib_in[j, i])

    def take_stat(d, carry):
        stat_from(d).wait_recv()
        return carry

    lax.fori_loop(1, total_devices, take_stat, 0)

    def total_of(i, carry):
        return carry[0] + stats[2 * i], carry[1] + stats[2 * i + 1]

    zero = jnp.zeros((PARTS, width), jnp.float32)
    even, odd = lax.fori_loop(0, total_devices // 2, total_of, (zero, zero))
    totals_ref[0] = even
    totals_ref[1] = odd

    for mk, cond in sent:
        when(cond, lambda: mk().wait_send())

    def done_stat(d, carry):
        stat(d).wait_send()
        return carry

    lax.fori_loop(1, total_devices, done_stat, 0)


def fused(blocks, owners, places, panel_matrix):
    R = lax.axis_size("row")
    C = lax.axis_size("col")
    S, BS, _ = blocks.shape
    CB, slab_rows, PW = panel_matrix.shape
    RB = CB * C // R
    width = PW // 2 // PARTS
    group = 2 * CB
    n_a = 11 * group // 16
    quarter = RB // CHIPS
    table = slot_table(owners, places, CB, RB)
    dma = lambda n: pltpu.SemaphoreType.DMA((n,))
    f32, bf16 = jnp.float32, blocks.dtype
    cfg = (R, S, CB, RB, BS, width, n_a)
    squares, totals = pl.pallas_call(
        functools.partial(panel_kernel, cfg),
        out_shape=(
            jax.ShapeDtypeStruct((quarter // 2 * BS, PW), f32),
            jax.ShapeDtypeStruct((2, PARTS, width), f32),
        ),
        in_specs=[pl.BlockSpec(memory_space=pl.ANY)] * 3,
        out_specs=[pl.BlockSpec(memory_space=pltpu.VMEM)] * 2,
        scratch_shapes=[
            pltpu.VMEM((CHIPS, group, BS, width), bf16),
            pltpu.VMEM((CHIPS, group, BS, width), bf16),
            pltpu.VMEM((S + 1, BS, BS), bf16),
            pltpu.VMEM((S + 1, BS, BS), bf16),
            pltpu.SMEM((8, 128), jnp.int32),
            pltpu.SMEM((8, 128), jnp.int32),
            pltpu.VMEM((8, 128), jnp.int32),
            pltpu.VMEM((S + RB + 1, BS, width), f32),
            pltpu.VMEM((PARTS, quarter, BS, width), f32),
            pltpu.VMEM((3, quarter, BS, width), jnp.int16),
            pltpu.VMEM((3, quarter, BS, width), jnp.int16),
            pltpu.VMEM((3, quarter, BS, width), jnp.int16),
            pltpu.VMEM((3, quarter, BS, width), jnp.int16),
            pltpu.VMEM((PARTS * 3, quarter, width), f32),
            pltpu.VMEM((PARTS * 3, quarter, width), f32),
            pltpu.VMEM((PARTS, quarter // 2, BS, width), f32),
            pltpu.VMEM((PARTS, quarter // 2, BS, width), f32),
            pltpu.VMEM((PARTS, quarter // 2, BS, width), f32),
            pltpu.VMEM((R * C, PARTS, width), f32),
            dma(5), dma(4), dma(4),
            dma(PARTS * 2 * R), dma(PARTS * 2 * R), dma(PARTS * 2 * R), dma(PARTS * 2 * R),
            dma(PARTS * 2 * R), dma(PARTS * 2 * R), dma(PARTS * 2 * R), dma(PARTS * 2 * R),
            dma(PARTS * 2), dma(PARTS * 2), dma(PARTS * 2), dma(PARTS * 2),
            dma(PARTS * 3), dma(PARTS * 3), dma(PARTS * 3), dma(PARTS * 3), dma(PARTS), dma(PARTS), dma(R * C), dma(R * C),
        ],
        compiler_params=pltpu.CompilerParams(
            collective_id=0, has_side_effects=True, vmem_limit_bytes=60 << 20
        ),
        cost_estimate=pl.CostEstimate(
            flops=2 * S * BS * BS * PW, bytes_accessed=4 << 20, transcendentals=0
        ),
    )(blocks, table, panel_matrix)
    col_mean = totals.reshape(PW) / (CB * C * BS)
    return squares / (col_mean + epsilon)


def on_device(blocks, owners, places, panel_matrix):
    col_count = lax.axis_size("col")
    row_count = lax.axis_size("row")
    col_blocks = panel_matrix.shape[0]
    block_side = blocks.shape[1]
    panel_width = panel_matrix.shape[2]
    row_blocks = col_blocks * col_count // row_count
    capacity = row_blocks * col_blocks // col_count
    targets = jnp.arange(col_count, dtype=jnp.int32)
    onehot = (owners[:, None] == targets[None, :]).astype(jnp.int32)
    before = jnp.cumsum(onehot, axis=0) - onehot
    bucket_rank = jnp.sum(before * onehot, axis=1)
    slot_index = owners * capacity + bucket_rank
    received = col_count * capacity
    outgoing = (
        jnp.zeros((received, block_side, block_side), blocks.dtype).at[slot_index].set(blocks)
    )
    out_places = jnp.zeros((received,), jnp.int32).at[slot_index].set(places)
    outgoing = outgoing.reshape(col_count, capacity, block_side, block_side)
    out_places = out_places.reshape(col_count, capacity)
    arrived, arrived_places = (
        lax.all_to_all(outgoing, "col", split_axis=0, concat_axis=0, tiled=True),
        lax.all_to_all(out_places, "col", split_axis=0, concat_axis=0, tiled=True),
    )
    arrived = arrived.reshape(received, block_side, block_side)
    arrived_places = arrived_places.reshape(received)
    row_in = arrived_places // col_blocks
    col_in = arrived_places % col_blocks
    panel_full = lax.all_gather(panel_matrix, "row", axis=1, tiled=True)
    group_size = min(32, received)
    turn_count = received // group_size

    def add_group(partial_value, members):
        tile_group, group_rows, group_cols = members
        pieces = panel_full[group_cols]
        product = jnp.einsum("sab,sbp->sap", tile_group, pieces, preferred_element_type=jnp.float32)
        return (partial_value.at[group_rows].add(product), None)

    start_sum = jnp.zeros((row_blocks, block_side, panel_width), jnp.float32)
    partial_value = lax.scan(
        add_group,
        start_sum,
        (
            arrived.reshape(turn_count, group_size, block_side, block_side),
            row_in.reshape(turn_count, group_size),
            col_in.reshape(turn_count, group_size),
        ),
    )[0]
    partial_rows = partial_value.reshape(row_blocks * block_side, panel_width)
    own_rows = lax.psum_scatter(partial_rows, "col", scatter_dimension=0, tiled=True)
    squares = own_rows * own_rows
    totals = lax.psum(jnp.sum(squares, axis=0), ("row", "col"))
    col_mean = totals / (col_blocks * col_count * block_side)
    return squares / (col_mean + epsilon)


def solution(mesh):
    fits = mesh.shape["col"] == 2 * CHIPS and mesh.shape["row"] == 4
    placed = (
        P(("row", "col"), None, None),
        P(("row", "col")),
        P(("row", "col")),
        P("col", "row", None),
    )
    return jax.shard_map(
        fused if fits else on_device, mesh=mesh, in_specs=placed, out_specs=P(("row", "col"), None), check_vma=False
    )
```

```python
import functools

import jax
import jax.numpy as jnp
from jax import lax
from jax.experimental import pallas as pl
from jax.experimental.pallas import tpu as pltpu
from jax.sharding import PartitionSpec as P

epsilon = 1e-06
CHIPS = 4
PARTS = 2
UNROLL = 8
LEVELS = 32767.0
smallest = 1e-30
MESH = pl.DeviceIdType.MESH


def slot_table(owners, places, col_blocks, row_blocks):
    count = owners.shape[0]
    ids = jnp.arange(count, dtype=jnp.int32)
    rows = places // col_blocks
    cols = owners * col_blocks + places % col_blocks
    targets = jnp.arange(row_blocks, dtype=jnp.int32)
    member = (rows[None, :] == targets[:, None]).astype(jnp.int32)
    held = jnp.sum(member, axis=1)
    filled = held + held % 2
    below = (targets[None, :] < targets[:, None]).astype(jnp.int32)
    base = jnp.sum(below * filled[None, :], axis=1)
    earlier = jnp.logical_and(rows[None, :] == rows[:, None], ids[None, :] < ids[:, None])
    rank = jnp.sum(earlier.astype(jnp.int32), axis=1)
    at = rank + jnp.sum(member * base[:, None], axis=0)
    entries = jnp.arange(count + row_blocks, dtype=jnp.int32)
    chosen = (at[None, :] == entries[:, None]).astype(jnp.int32)
    code = jnp.sum(chosen * (cols * 2 * count + ids - count)[None, :], axis=1) + count
    pairs = entries[: entries.shape[0] // 2]
    starts = jnp.logical_and(base[None, :] == 2 * pairs[:, None], held[None, :] > 0)
    first = jnp.any(starts, axis=1).astype(jnp.int32)
    last = jnp.where(held > 0, (base + filled) // 2, 0)
    lines = [jnp.pad(v, (0, 128 - v.shape[0])) for v in (code, first, last)]
    return jnp.stack(lines + [jnp.zeros((128,), jnp.int32)] * 5)


def panel_kernel(
    cfg,
    blocks_ref, table_ref, panel_ref,
    squares_ref, totals_ref,
    pan0, pan1, own_blocks, sib_blocks, own_table, sib_table, sib_table_vmem,
    run, part, code0, code1, arrive0, arrive1, scale_out, scale_in, sib_in, sib_out, mine, stats,
    local_sem, pair_send, pair_recv,
    za_send, za_recv, zb_send, zb_recv,
    xa_send, xa_recv, ra_send, ra_recv,
    xb_send, xb_recv, rb_send, rb_recv,
    rs_send, rs_recv, sc_send, sc_recv, out_send, out_recv, st_send, st_recv,
):
    R, S, CB, RB, BS, width, n_a = cfg
    C = 2 * CHIPS
    slab_rows = BS // R
    group = 2 * CB
    pairs = (S + RB) // 2
    quarter = RB // CHIPS
    own_rows = quarter // 2
    pans, codes, arrives = (pan0, pan1), (code0, code1), (arrive0, arrive1)
    z = lax.axis_index("row")
    c = lax.axis_index("col")
    q = c // 2
    k = c % 2
    qx = q + 1 - 2 * (q % 2)
    qy = lax.rem(q + 2, 4)
    qd = 3 - q
    me = z * C + c
    total_devices = R * C
    nbrs = (qx, qy)
    sent = []

    def true():
        return None

    def when(cond, f):
        if cond is None:
            f()
        else:
            pl.when(cond)(f)

    def start(mk, cond=None):
        when(cond, lambda: mk().start())
        sent.append((mk, cond))

    def remote(src, dst, s, r, dev):
        return pltpu.make_async_remote_copy(
            src_ref=src, dst_ref=dst, send_sem=s, recv_sem=r, device_id=dev, device_id_type=MESH
        )

    barrier = pltpu.get_barrier_semaphore()

    def greet(d, carry):
        t = lax.rem(me + d, total_devices)
        pl.semaphore_signal(barrier, inc=1, device_id=(t // C, t % C), device_id_type=MESH)
        return carry

    lax.fori_loop(1, total_devices, greet, 0)

    def slab(zz):
        return pl.ds(pl.multiple_of(zz * slab_rows, slab_rows), slab_rows)

    def local(i, src, dst):
        return pltpu.make_async_copy(src, dst, local_sem.at[i])

    def panel_cols(core, j):
        return pl.ds(pl.multiple_of((core * PARTS + j) * width, width), width)

    for j in range(PARTS):
        local(
            j, panel_ref.at[:, :, panel_cols(k, j)],
            pans[j].at[q, pl.ds(k * CB, CB), slab(z)],
        ).start()
    local(2, table_ref, own_table).start()
    local(3, blocks_ref, own_blocks.at[pl.ds(0, S)]).start()
    pl.semaphore_wait(barrier, total_devices - 1)

    sib = (z, q * 2 + 1 - k)

    def pair_panel(j):
        return remote(
            panel_ref.at[:, :, panel_cols(1 - k, j)],
            pans[j].at[q, pl.ds(k * CB, CB), slab(z)],
            pair_send.at[j], pair_recv.at[j], sib,
        )

    for j in range(PARTS):
        start(functools.partial(pair_panel, j))

    def pair_table():
        return remote(table_ref, sib_table_vmem, pair_send.at[2], pair_recv.at[2], sib)

    def pair_blocks():
        return remote(blocks_ref, sib_blocks.at[pl.ds(0, S)], pair_send.at[3], pair_recv.at[3], sib)

    start(pair_table)
    start(pair_blocks)

    def dev_q(qq):
        return (z, qq * 2 + k)

    def a_range(part):
        half = n_a // 2
        return (pl.ds(0, n_a), pl.ds(0, half), pl.ds(half, n_a - half))[part]

    def b_range(part):
        n_b = group - n_a
        half = n_b // 2
        return (pl.ds(n_a, n_b), pl.ds(n_a, half), pl.ds(n_a + half, n_b - half))[part]

    def za(j, up, d):
        shard = z - (d - 1) if up else z + (d - 1)
        view = pans[j].at[q, a_range(0), slab(jnp.clip(shard, 0, R - 1))]
        i = (j * 2 + up) * R + d - 1
        to = jnp.clip(z + 1 if up else z - 1, 0, R - 1)
        return remote(view, view, za_send.at[i], za_recv.at[i], (to, c))

    def zb(j, up, d):
        shard = z - (d - 1) if up else z + (d - 1)
        view = pans[j].at[:, b_range(0), slab(jnp.clip(shard, 0, R - 1))]
        i = (j * 2 + up) * R + d - 1
        to = jnp.clip(z + 1 if up else z - 1, 0, R - 1)
        return remote(view, view, zb_send.at[i], zb_recv.at[i], (to, c))

    def z_send_cond(up, d):
        if up:
            return jnp.logical_and(z - (d - 1) >= 0, z + 1 < R)
        return jnp.logical_and(z + (d - 1) < R, z - 1 >= 0)

    def z_recv_cond(up, d):
        return z - d >= 0 if up else z + d < R

    def z_from(up, d):
        return jnp.clip(z - d if up else z + d, 0, R - 1)

    def xa(j, n, zz):
        view = pans[j].at[q, a_range(0), slab(zz)]
        i = (j * 2 + n) * R + zz
        return remote(view, view, xa_send.at[i], xa_recv.at[i], dev_q(nbrs[n]))

    def ra(j, n, zz):
        view = pans[j].at[nbrs[n], a_range(1 + n), slab(zz)]
        i = (j * 2 + n) * R + zz
        return remote(view, view, ra_send.at[i], ra_recv.at[i], dev_q(nbrs[1 - n]))

    def xb(j, n):
        view = pans[j].at[q, b_range(0), slab(z)]
        i = j * 2 + n
        return remote(view, view, xb_send.at[i], xb_recv.at[i], dev_q(nbrs[n]))

    def rb(j, n):
        view = pans[j].at[nbrs[n], b_range(1 + n), slab(z)]
        i = j * 2 + n
        return remote(view, view, rb_send.at[i], rb_recv.at[i], dev_q(nbrs[1 - n]))

    p = functools.partial

    def gather_step(j, s):
        if s == 0:
            local(
                j, panel_ref.at[:, :, panel_cols(k, j)],
                pans[j].at[q, pl.ds(k * CB, CB), slab(z)],
            ).wait()
            pair_panel(j).wait_recv()
            for up in (1, 0):
                start(p(za, j, up, 1), z_send_cond(up, 1))
            for n in (0, 1):
                start(p(xb, j, n))
            for n in (0, 1):
                start(p(xa, j, n, z))
            return
        if s == 1:
            for n in (0, 1):
                xb(j, n).wait_recv()
                start(p(rb, j, n))
        if s == 2:
            for n in (0, 1):
                rb(j, n).wait_recv()
            for up in (1, 0):
                start(p(zb, j, up, 1), z_send_cond(up, 1))
        if s < R:
            for up in (1, 0):
                cond = z_recv_cond(up, s)
                when(cond, lambda: za(j, up, s).wait_recv())
                if s < R - 1:
                    start(p(za, j, up, s + 1), z_send_cond(up, s + 1))
                for n in (0, 1):
                    start(p(xa, j, n, z_from(up, s)), cond)
        if 1 <= s <= R:
            d = s - 1
            for up in (1, 0) if d else (1,):
                cond = z_recv_cond(up, d) if d else None
                zz = z_from(up, d)
                for n in (0, 1):
                    when(cond, lambda: xa(j, n, zz).wait_recv())
                    start(p(ra, j, n, zz), cond)
        if s >= 3:
            d = s - 2
            for up in (1, 0):
                when(z_recv_cond(up, d), lambda: zb(j, up, d).wait_recv())
                if d < R - 1:
                    start(p(zb, j, up, d + 1), z_send_cond(up, d + 1))
        if s == steps - 1:
            for zz in range(R):
                for n in (0, 1):
                    ra(j, n, zz).wait_recv()

    steps = R + 2

    def multiply(j, blocks, table, base):
        pan = pans[j]

        def turn(g, acc):
            for u in range(UNROLL):
                t = g * UNROLL + u
                tiles, pieces = [], []
                for e in (0, 1):
                    code = table[0, 2 * t + e]
                    col = lax.div(code, 2 * S)
                    tiles.append(blocks[lax.rem(code, 2 * S)])
                    pieces.append(pan[lax.div(col, group), lax.rem(col, group)])
                product = jnp.dot(
                    jnp.concatenate(tiles, axis=1), jnp.concatenate(pieces, axis=0),
                    preferred_element_type=jnp.float32,
                )
                acc = jnp.where(table[1, t] == 1, 0.0, acc) + product
                run[base + t] = acc
            return acc

        lax.fori_loop(0, pairs // UNROLL, turn, jnp.zeros((BS, width), jnp.float32))

    others = (qx, qy, qd)

    def scatter(j, rel):
        i = j * 3 + rel
        return remote(
            codes[j].at[rel], arrives[j].at[rel], rs_send.at[i], rs_recv.at[i],
            dev_q(others[rel]),
        )

    def scatter_scale(j, rel):
        i = j * 3 + rel
        return remote(
            scale_out.at[i], scale_in.at[i], sc_send.at[i], sc_recv.at[i], dev_q(others[rel])
        )

    def row_sum(i):
        a = own_table[2, i]
        b = sib_table[2, i]
        b = jnp.where(b > 0, b + pairs, 0)
        return run[a] + run[b]

    def add_rows(j):
        for rel in (2, 0, 1):
            for b in range(quarter):
                value = row_sum(others[rel] * quarter + b)
                top = jnp.max(jnp.abs(value), axis=0, keepdims=True)
                top = jnp.maximum(top, smallest)
                codes[j][rel, b] = jnp.round(value * (LEVELS / top)).astype(jnp.int32).astype(jnp.int16)
                scale_out[j * 3 + rel, pl.ds(b, 1)] = top * (1.0 / LEVELS)
            start(p(scatter_scale, j, rel))
            start(p(scatter, j, rel))
        for b in range(quarter):
            part[j, b] = row_sum(q * quarter + b)

    def pair_rows(j):
        return remote(sib_out.at[j], sib_in.at[j], out_send.at[j], out_recv.at[j], sib)

    def square(j):
        for rel in range(3):
            scatter_scale(j, rel).wait_recv()
            scatter(j, rel).wait_recv()

        def block(b, total, keep):
            value = part[j, b]
            for rel in range(3):
                code = arrives[j][rel, b].astype(jnp.int32).astype(jnp.float32)
                value = value + code * scale_in[j * 3 + rel, pl.ds(b, 1)]
            value = value * value
            keep(value)
            return total + jnp.sum(value.reshape(BS // 8, 8, width), axis=0)

        total = jnp.zeros((8, width), jnp.float32)
        for i in range(own_rows):
            def keep(value):
                sib_out[j, i] = value
            total = block((1 - k) * own_rows + i, total, keep)
        start(p(pair_rows, j))
        for i in range(own_rows):
            def keep_mine(value):
                mine[j, i] = value
            total = block(k * own_rows + i, total, keep_mine)
        stats[me, pl.ds(j, 1)] = jnp.sum(total, axis=0, keepdims=True)

    lag = 2
    for s in range(steps):
        gather_step(0, s)
        if s >= lag:
            gather_step(1, s - lag)
    local(2, table_ref, own_table).wait()
    local(3, blocks_ref, own_blocks.at[pl.ds(0, S)]).wait()
    pair_table().wait_recv()
    local(4, sib_table_vmem, sib_table).start()
    run[0] = jnp.zeros((BS, width), jnp.float32)
    for held in (own_blocks, sib_blocks):
        held[S] = jnp.zeros((BS, BS), held.dtype)
    local(4, sib_table_vmem, sib_table).wait()
    pair_blocks().wait_recv()
    multiply(0, own_blocks, own_table, 1)
    gather_step(1, steps - 2)
    multiply(0, sib_blocks, sib_table, 1 + pairs)
    add_rows(0)
    gather_step(1, steps - 1)
    multiply(1, own_blocks, own_table, 1)
    multiply(1, sib_blocks, sib_table, 1 + pairs)
    add_rows(1)
    square(0)
    square(1)

    def stat(d):
        t = lax.rem(me + d, total_devices)
        return remote(
            stats.at[me], stats.at[me], st_send.at[t], st_recv.at[me], (t // C, t % C)
        )

    def stat_from(d):
        t = lax.rem(me + d, total_devices)
        return remote(
            stats.at[t], stats.at[t], st_send.at[t], st_recv.at[t], (t // C, t % C)
        )

    def send_stat(d, carry):
        stat(d).start()
        return carry

    lax.fori_loop(1, total_devices, send_stat, 0)

    def put(j, core, value_of):
        for i in range(own_rows):
            squares_ref[pl.ds(i * BS, BS), panel_cols(core, j)] = value_of(i)

    for j in range(PARTS):
        put(j, k, lambda i: mine[j, i])
    for j in range(PARTS):
        pair_rows(j).wait_recv()
        put(j, 1 - k, lambda i: sib_in[j, i])

    def take_stat(d, carry):
        stat_from(d).wait_recv()
        return carry

    lax.fori_loop(1, total_devices, take_stat, 0)

    def total_of(i, carry):
        return carry[0] + stats[2 * i], carry[1] + stats[2 * i + 1]

    zero = jnp.zeros((PARTS, width), jnp.float32)
    even, odd = lax.fori_loop(0, total_devices // 2, total_of, (zero, zero))
    totals_ref[0] = even
    totals_ref[1] = odd

    for mk, cond in sent:
        when(cond, lambda: mk().wait_send())

    def done_stat(d, carry):
        stat(d).wait_send()
        return carry

    lax.fori_loop(1, total_devices, done_stat, 0)


def fused(blocks, owners, places, panel_matrix):
    R = lax.axis_size("row")
    C = lax.axis_size("col")
    S, BS, _ = blocks.shape
    CB, slab_rows, PW = panel_matrix.shape
    RB = CB * C // R
    width = PW // 2 // PARTS
    group = 2 * CB
    n_a = 14 * group // 16
    quarter = RB // CHIPS
    table = slot_table(owners, places, CB, RB)
    dma = lambda n: pltpu.SemaphoreType.DMA((n,))
    f32, bf16 = jnp.float32, blocks.dtype
    cfg = (R, S, CB, RB, BS, width, n_a)
    squares, totals = pl.pallas_call(
        functools.partial(panel_kernel, cfg),
        out_shape=(
            jax.ShapeDtypeStruct((quarter // 2 * BS, PW), f32),
            jax.ShapeDtypeStruct((2, PARTS, width), f32),
        ),
        in_specs=[pl.BlockSpec(memory_space=pl.ANY)] * 3,
        out_specs=[pl.BlockSpec(memory_space=pltpu.VMEM)] * 2,
        scratch_shapes=[
            pltpu.VMEM((CHIPS, group, BS, width), bf16),
            pltpu.VMEM((CHIPS, group, BS, width), bf16),
            pltpu.VMEM((S + 1, BS, BS), bf16),
            pltpu.VMEM((S + 1, BS, BS), bf16),
            pltpu.SMEM((8, 128), jnp.int32),
            pltpu.SMEM((8, 128), jnp.int32),
            pltpu.VMEM((8, 128), jnp.int32),
            pltpu.VMEM((S + RB + 1, BS, width), f32),
            pltpu.VMEM((PARTS, quarter, BS, width), f32),
            pltpu.VMEM((3, quarter, BS, width), jnp.int16),
            pltpu.VMEM((3, quarter, BS, width), jnp.int16),
            pltpu.VMEM((3, quarter, BS, width), jnp.int16),
            pltpu.VMEM((3, quarter, BS, width), jnp.int16),
            pltpu.VMEM((PARTS * 3, quarter, width), f32),
            pltpu.VMEM((PARTS * 3, quarter, width), f32),
            pltpu.VMEM((PARTS, quarter // 2, BS, width), f32),
            pltpu.VMEM((PARTS, quarter // 2, BS, width), f32),
            pltpu.VMEM((PARTS, quarter // 2, BS, width), f32),
            pltpu.VMEM((R * C, PARTS, width), f32),
            dma(5), dma(4), dma(4),
            dma(PARTS * 2 * R), dma(PARTS * 2 * R), dma(PARTS * 2 * R), dma(PARTS * 2 * R),
            dma(PARTS * 2 * R), dma(PARTS * 2 * R), dma(PARTS * 2 * R), dma(PARTS * 2 * R),
            dma(PARTS * 2), dma(PARTS * 2), dma(PARTS * 2), dma(PARTS * 2),
            dma(PARTS * 3), dma(PARTS * 3), dma(PARTS * 3), dma(PARTS * 3), dma(PARTS), dma(PARTS), dma(R * C), dma(R * C),
        ],
        compiler_params=pltpu.CompilerParams(
            collective_id=0, has_side_effects=True, vmem_limit_bytes=60 << 20
        ),
        cost_estimate=pl.CostEstimate(
            flops=2 * S * BS * BS * PW, bytes_accessed=4 << 20, transcendentals=0
        ),
    )(blocks, table, panel_matrix)
    col_mean = totals.reshape(PW) / (CB * C * BS)
    return squares / (col_mean + epsilon)


def on_device(blocks, owners, places, panel_matrix):
    col_count = lax.axis_size("col")
    row_count = lax.axis_size("row")
    col_blocks = panel_matrix.shape[0]
    block_side = blocks.shape[1]
    panel_width = panel_matrix.shape[2]
    row_blocks = col_blocks * col_count // row_count
    capacity = row_blocks * col_blocks // col_count
    targets = jnp.arange(col_count, dtype=jnp.int32)
    onehot = (owners[:, None] == targets[None, :]).astype(jnp.int32)
    before = jnp.cumsum(onehot, axis=0) - onehot
    bucket_rank = jnp.sum(before * onehot, axis=1)
    slot_index = owners * capacity + bucket_rank
    received = col_count * capacity
    outgoing = (
        jnp.zeros((received, block_side, block_side), blocks.dtype).at[slot_index].set(blocks)
    )
    out_places = jnp.zeros((received,), jnp.int32).at[slot_index].set(places)
    outgoing = outgoing.reshape(col_count, capacity, block_side, block_side)
    out_places = out_places.reshape(col_count, capacity)
    arrived, arrived_places = (
        lax.all_to_all(outgoing, "col", split_axis=0, concat_axis=0, tiled=True),
        lax.all_to_all(out_places, "col", split_axis=0, concat_axis=0, tiled=True),
    )
    arrived = arrived.reshape(received, block_side, block_side)
    arrived_places = arrived_places.reshape(received)
    row_in = arrived_places // col_blocks
    col_in = arrived_places % col_blocks
    panel_full = lax.all_gather(panel_matrix, "row", axis=1, tiled=True)
    group_size = min(32, received)
    turn_count = received // group_size

    def add_group(partial_value, members):
        tile_group, group_rows, group_cols = members
        pieces = panel_full[group_cols]
        product = jnp.einsum("sab,sbp->sap", tile_group, pieces, preferred_element_type=jnp.float32)
        return (partial_value.at[group_rows].add(product), None)

    start_sum = jnp.zeros((row_blocks, block_side, panel_width), jnp.float32)
    partial_value = lax.scan(
        add_group,
        start_sum,
        (
            arrived.reshape(turn_count, group_size, block_side, block_side),
            row_in.reshape(turn_count, group_size),
            col_in.reshape(turn_count, group_size),
        ),
    )[0]
    partial_rows = partial_value.reshape(row_blocks * block_side, panel_width)
    own_rows = lax.psum_scatter(partial_rows, "col", scatter_dimension=0, tiled=True)
    squares = own_rows * own_rows
    totals = lax.psum(jnp.sum(squares, axis=0), ("row", "col"))
    col_mean = totals / (col_blocks * col_count * block_side)
    return squares / (col_mean + epsilon)


def solution(mesh):
    fits = mesh.shape["col"] == 2 * CHIPS and mesh.shape["row"] == 4
    placed = (
        P(("row", "col"), None, None),
        P(("row", "col")),
        P(("row", "col")),
        P("col", "row", None),
    )
    return jax.shard_map(
        fused if fits else on_device, mesh=mesh, in_specs=placed, out_specs=P(("row", "col"), None), check_vma=False
    )
```

```python
import functools

import jax
import jax.numpy as jnp
from jax import lax
from jax.experimental import pallas as pl
from jax.experimental.pallas import tpu as pltpu
from jax.sharding import PartitionSpec as P

epsilon = 1e-06
CHIPS = 4
PARTS = 2
UNROLL = 8
LEVELS = 32767.0
smallest = 1e-30
MESH = pl.DeviceIdType.MESH


def slot_table(owners, places, col_blocks, row_blocks):
    count = owners.shape[0]
    ids = jnp.arange(count, dtype=jnp.int32)
    rows = places // col_blocks
    cols = owners * col_blocks + places % col_blocks
    targets = jnp.arange(row_blocks, dtype=jnp.int32)
    member = (rows[None, :] == targets[:, None]).astype(jnp.int32)
    held = jnp.sum(member, axis=1)
    filled = held + held % 2
    below = (targets[None, :] < targets[:, None]).astype(jnp.int32)
    base = jnp.sum(below * filled[None, :], axis=1)
    earlier = jnp.logical_and(rows[None, :] == rows[:, None], ids[None, :] < ids[:, None])
    rank = jnp.sum(earlier.astype(jnp.int32), axis=1)
    at = rank + jnp.sum(member * base[:, None], axis=0)
    entries = jnp.arange(count + row_blocks, dtype=jnp.int32)
    chosen = (at[None, :] == entries[:, None]).astype(jnp.int32)
    code = jnp.sum(chosen * (cols * 2 * count + ids - count)[None, :], axis=1) + count
    pairs = entries[: entries.shape[0] // 2]
    starts = jnp.logical_and(base[None, :] == 2 * pairs[:, None], held[None, :] > 0)
    first = jnp.any(starts, axis=1).astype(jnp.int32)
    last = jnp.where(held > 0, (base + filled) // 2, 0)
    lines = [jnp.pad(v, (0, 128 - v.shape[0])) for v in (code, first, last)]
    return jnp.stack(lines + [jnp.zeros((128,), jnp.int32)] * 5)


def panel_kernel(
    cfg,
    blocks_ref, table_ref, panel_ref,
    squares_ref, totals_ref,
    pan0, pan1, own_blocks, sib_blocks, own_table, sib_table, sib_table_vmem,
    run, part, code0, code1, arrive0, arrive1, scale_out, scale_in, sib_in, sib_out, mine, stats,
    local_sem, pair_send, pair_recv,
    za_send, za_recv, zb_send, zb_recv,
    xa_send, xa_recv, ra_send, ra_recv,
    xb_send, xb_recv, rb_send, rb_recv,
    rs_send, rs_recv, sc_send, sc_recv, out_send, out_recv, st_send, st_recv,
):
    R, S, CB, RB, BS, width, n_a = cfg
    C = 2 * CHIPS
    slab_rows = BS // R
    group = 2 * CB
    pairs = (S + RB) // 2
    quarter = RB // CHIPS
    own_rows = quarter // 2
    pans, codes, arrives = (pan0, pan1), (code0, code1), (arrive0, arrive1)
    z = lax.axis_index("row")
    c = lax.axis_index("col")
    q = c // 2
    k = c % 2
    qx = q + 1 - 2 * (q % 2)
    qy = lax.rem(q + 2, 4)
    qd = 3 - q
    me = z * C + c
    total_devices = R * C
    nbrs = (qx, qy)
    sent = []

    def true():
        return None

    def when(cond, f):
        if cond is None:
            f()
        else:
            pl.when(cond)(f)

    def start(mk, cond=None):
        when(cond, lambda: mk().start())
        sent.append((mk, cond))

    def remote(src, dst, s, r, dev):
        return pltpu.make_async_remote_copy(
            src_ref=src, dst_ref=dst, send_sem=s, recv_sem=r, device_id=dev, device_id_type=MESH
        )

    barrier = pltpu.get_barrier_semaphore()

    def greet(d, carry):
        t = lax.rem(me + d, total_devices)
        pl.semaphore_signal(barrier, inc=1, device_id=(t // C, t % C), device_id_type=MESH)
        return carry

    lax.fori_loop(1, total_devices, greet, 0)

    def slab(zz):
        return pl.ds(pl.multiple_of(zz * slab_rows, slab_rows), slab_rows)

    def local(i, src, dst):
        return pltpu.make_async_copy(src, dst, local_sem.at[i])

    def panel_cols(core, j):
        return pl.ds(pl.multiple_of((core * PARTS + j) * width, width), width)

    for j in range(PARTS):
        local(
            j, panel_ref.at[:, :, panel_cols(k, j)],
            pans[j].at[q, pl.ds(k * CB, CB), slab(z)],
        ).start()
    local(2, table_ref, own_table).start()
    pl.semaphore_wait(barrier, total_devices - 1)

    sib = (z, q * 2 + 1 - k)

    def pair_panel(j):
        return remote(
            panel_ref.at[:, :, panel_cols(1 - k, j)],
            pans[j].at[q, pl.ds(k * CB, CB), slab(z)],
            pair_send.at[j], pair_recv.at[j], sib,
        )

    for j in range(PARTS):
        start(functools.partial(pair_panel, j))

    def pair_table():
        return remote(table_ref, sib_table_vmem, pair_send.at[2], pair_recv.at[2], sib)

    def pair_blocks():
        return remote(blocks_ref, sib_blocks.at[pl.ds(0, S)], pair_send.at[3], pair_recv.at[3], sib)

    start(pair_table)

    def dev_q(qq):
        return (z, qq * 2 + k)

    def a_range(part):
        half = n_a // 2
        return (pl.ds(0, n_a), pl.ds(0, half), pl.ds(half, n_a - half))[part]

    def b_range(part):
        n_b = group - n_a
        half = n_b // 2
        return (pl.ds(n_a, n_b), pl.ds(n_a, half), pl.ds(n_a + half, n_b - half))[part]

    def za(j, up, d):
        shard = z - (d - 1) if up else z + (d - 1)
        view = pans[j].at[q, a_range(0), slab(jnp.clip(shard, 0, R - 1))]
        i = (j * 2 + up) * R + d - 1
        to = jnp.clip(z + 1 if up else z - 1, 0, R - 1)
        return remote(view, view, za_send.at[i], za_recv.at[i], (to, c))

    def zb(j, up, d):
        shard = z - (d - 1) if up else z + (d - 1)
        view = pans[j].at[:, b_range(0), slab(jnp.clip(shard, 0, R - 1))]
        i = (j * 2 + up) * R + d - 1
        to = jnp.clip(z + 1 if up else z - 1, 0, R - 1)
        return remote(view, view, zb_send.at[i], zb_recv.at[i], (to, c))

    def z_send_cond(up, d):
        if up:
            return jnp.logical_and(z - (d - 1) >= 0, z + 1 < R)
        return jnp.logical_and(z + (d - 1) < R, z - 1 >= 0)

    def z_recv_cond(up, d):
        return z - d >= 0 if up else z + d < R

    def z_from(up, d):
        return jnp.clip(z - d if up else z + d, 0, R - 1)

    def xa(j, n, zz):
        view = pans[j].at[q, a_range(0), slab(zz)]
        i = (j * 2 + n) * R + zz
        return remote(view, view, xa_send.at[i], xa_recv.at[i], dev_q(nbrs[n]))

    def ra(j, n, zz):
        view = pans[j].at[nbrs[n], a_range(1 + n), slab(zz)]
        i = (j * 2 + n) * R + zz
        return remote(view, view, ra_send.at[i], ra_recv.at[i], dev_q(nbrs[1 - n]))

    def xb(j, n):
        view = pans[j].at[q, b_range(0), slab(z)]
        i = j * 2 + n
        return remote(view, view, xb_send.at[i], xb_recv.at[i], dev_q(nbrs[n]))

    def rb(j, n):
        view = pans[j].at[nbrs[n], b_range(1 + n), slab(z)]
        i = j * 2 + n
        return remote(view, view, rb_send.at[i], rb_recv.at[i], dev_q(nbrs[1 - n]))

    p = functools.partial

    def gather_step(j, s):
        if s == 0:
            local(
                j, panel_ref.at[:, :, panel_cols(k, j)],
                pans[j].at[q, pl.ds(k * CB, CB), slab(z)],
            ).wait()
            pair_panel(j).wait_recv()
            for up in (1, 0):
                start(p(za, j, up, 1), z_send_cond(up, 1))
            for n in (0, 1):
                start(p(xb, j, n))
            for n in (0, 1):
                start(p(xa, j, n, z))
            return
        if s == 1:
            for n in (0, 1):
                xb(j, n).wait_recv()
                start(p(rb, j, n))
        if s == 2:
            for n in (0, 1):
                rb(j, n).wait_recv()
            for up in (1, 0):
                start(p(zb, j, up, 1), z_send_cond(up, 1))
        if s < R:
            for up in (1, 0):
                cond = z_recv_cond(up, s)
                when(cond, lambda: za(j, up, s).wait_recv())
                if s < R - 1:
                    start(p(za, j, up, s + 1), z_send_cond(up, s + 1))
                for n in (0, 1):
                    start(p(xa, j, n, z_from(up, s)), cond)
        if 1 <= s <= R:
            d = s - 1
            for up in (1, 0) if d else (1,):
                cond = z_recv_cond(up, d) if d else None
                zz = z_from(up, d)
                for n in (0, 1):
                    when(cond, lambda: xa(j, n, zz).wait_recv())
                    start(p(ra, j, n, zz), cond)
        if s >= 3:
            d = s - 2
            for up in (1, 0):
                when(z_recv_cond(up, d), lambda: zb(j, up, d).wait_recv())
                if d < R - 1:
                    start(p(zb, j, up, d + 1), z_send_cond(up, d + 1))
        if s == steps - 1:
            for zz in range(R):
                for n in (0, 1):
                    ra(j, n, zz).wait_recv()

    steps = R + 2

    def multiply(j, blocks, table, base):
        pan = pans[j]

        def turn(g, acc):
            for u in range(UNROLL):
                t = g * UNROLL + u
                tiles, pieces = [], []
                for e in (0, 1):
                    code = table[0, 2 * t + e]
                    col = lax.div(code, 2 * S)
                    tiles.append(blocks[lax.rem(code, 2 * S)])
                    pieces.append(pan[lax.div(col, group), lax.rem(col, group)])
                product = jnp.dot(
                    jnp.concatenate(tiles, axis=1), jnp.concatenate(pieces, axis=0),
                    preferred_element_type=jnp.float32,
                )
                acc = jnp.where(table[1, t] == 1, 0.0, acc) + product
                run[base + t] = acc
            return acc

        lax.fori_loop(0, pairs // UNROLL, turn, jnp.zeros((BS, width), jnp.float32))

    others = (qx, qy, qd)

    def scatter(j, rel):
        i = j * 3 + rel
        return remote(
            codes[j].at[rel], arrives[j].at[rel], rs_send.at[i], rs_recv.at[i],
            dev_q(others[rel]),
        )

    def scatter_scale(j, rel):
        i = j * 3 + rel
        return remote(
            scale_out.at[i], scale_in.at[i], sc_send.at[i], sc_recv.at[i], dev_q(others[rel])
        )

    def row_sum(i):
        a = own_table[2, i]
        b = sib_table[2, i]
        b = jnp.where(b > 0, b + pairs, 0)
        return run[a] + run[b]

    def add_rows(j):
        for rel in (2, 0, 1):
            for b in range(quarter):
                value = row_sum(others[rel] * quarter + b)
                top = jnp.max(jnp.abs(value), axis=0, keepdims=True)
                top = jnp.maximum(top, smallest)
                codes[j][rel, b] = jnp.round(value * (LEVELS / top)).astype(jnp.int32).astype(jnp.int16)
                scale_out[j * 3 + rel, pl.ds(b, 1)] = top * (1.0 / LEVELS)
            start(p(scatter_scale, j, rel))
            start(p(scatter, j, rel))
        for b in range(quarter):
            part[j, b] = row_sum(q * quarter + b)

    def pair_rows(j):
        return remote(sib_out.at[j], sib_in.at[j], out_send.at[j], out_recv.at[j], sib)

    def square(j):
        for rel in range(3):
            scatter_scale(j, rel).wait_recv()
            scatter(j, rel).wait_recv()

        def block(b, total, keep):
            value = part[j, b]
            for rel in range(3):
                code = arrives[j][rel, b].astype(jnp.int32).astype(jnp.float32)
                value = value + code * scale_in[j * 3 + rel, pl.ds(b, 1)]
            value = value * value
            keep(value)
            return total + jnp.sum(value.reshape(BS // 8, 8, width), axis=0)

        total = jnp.zeros((8, width), jnp.float32)
        for i in range(own_rows):
            def keep(value):
                sib_out[j, i] = value
            total = block((1 - k) * own_rows + i, total, keep)
        start(p(pair_rows, j))
        for i in range(own_rows):
            def keep_mine(value):
                mine[j, i] = value
            total = block(k * own_rows + i, total, keep_mine)
        stats[me, pl.ds(j, 1)] = jnp.sum(total, axis=0, keepdims=True)

    lag = 2
    for s in range(steps):
        gather_step(0, s)
        if s >= lag:
            gather_step(1, s - lag)
        if s == lag:
            start(pair_blocks)
            local(3, blocks_ref, own_blocks.at[pl.ds(0, S)]).start()
    local(2, table_ref, own_table).wait()
    local(3, blocks_ref, own_blocks.at[pl.ds(0, S)]).wait()
    pair_table().wait_recv()
    local(4, sib_table_vmem, sib_table).start()
    run[0] = jnp.zeros((BS, width), jnp.float32)
    for held in (own_blocks, sib_blocks):
        held[S] = jnp.zeros((BS, BS), held.dtype)
    local(4, sib_table_vmem, sib_table).wait()
    pair_blocks().wait_recv()
    multiply(0, own_blocks, own_table, 1)
    gather_step(1, steps - 2)
    multiply(0, sib_blocks, sib_table, 1 + pairs)
    add_rows(0)
    gather_step(1, steps - 1)
    multiply(1, own_blocks, own_table, 1)
    multiply(1, sib_blocks, sib_table, 1 + pairs)
    add_rows(1)
    square(0)
    square(1)

    def stat(d):
        t = lax.rem(me + d, total_devices)
        return remote(
            stats.at[me], stats.at[me], st_send.at[t], st_recv.at[me], (t // C, t % C)
        )

    def stat_from(d):
        t = lax.rem(me + d, total_devices)
        return remote(
            stats.at[t], stats.at[t], st_send.at[t], st_recv.at[t], (t // C, t % C)
        )

    def send_stat(d, carry):
        stat(d).start()
        return carry

    lax.fori_loop(1, total_devices, send_stat, 0)

    def put(j, core, value_of):
        for i in range(own_rows):
            squares_ref[pl.ds(i * BS, BS), panel_cols(core, j)] = value_of(i)

    for j in range(PARTS):
        put(j, k, lambda i: mine[j, i])
    for j in range(PARTS):
        pair_rows(j).wait_recv()
        put(j, 1 - k, lambda i: sib_in[j, i])

    def take_stat(d, carry):
        stat_from(d).wait_recv()
        return carry

    lax.fori_loop(1, total_devices, take_stat, 0)

    def total_of(i, carry):
        return carry[0] + stats[2 * i], carry[1] + stats[2 * i + 1]

    zero = jnp.zeros((PARTS, width), jnp.float32)
    even, odd = lax.fori_loop(0, total_devices // 2, total_of, (zero, zero))
    totals_ref[0] = even
    totals_ref[1] = odd

    for mk, cond in sent:
        when(cond, lambda: mk().wait_send())

    def done_stat(d, carry):
        stat(d).wait_send()
        return carry

    lax.fori_loop(1, total_devices, done_stat, 0)


def fused(blocks, owners, places, panel_matrix):
    R = lax.axis_size("row")
    C = lax.axis_size("col")
    S, BS, _ = blocks.shape
    CB, slab_rows, PW = panel_matrix.shape
    RB = CB * C // R
    width = PW // 2 // PARTS
    group = 2 * CB
    n_a = 12 * group // 16
    quarter = RB // CHIPS
    table = slot_table(owners, places, CB, RB)
    dma = lambda n: pltpu.SemaphoreType.DMA((n,))
    f32, bf16 = jnp.float32, blocks.dtype
    cfg = (R, S, CB, RB, BS, width, n_a)
    squares, totals = pl.pallas_call(
        functools.partial(panel_kernel, cfg),
        out_shape=(
            jax.ShapeDtypeStruct((quarter // 2 * BS, PW), f32),
            jax.ShapeDtypeStruct((2, PARTS, width), f32),
        ),
        in_specs=[pl.BlockSpec(memory_space=pl.ANY)] * 3,
        out_specs=[pl.BlockSpec(memory_space=pltpu.VMEM)] * 2,
        scratch_shapes=[
            pltpu.VMEM((CHIPS, group, BS, width), bf16),
            pltpu.VMEM((CHIPS, group, BS, width), bf16),
            pltpu.VMEM((S + 1, BS, BS), bf16),
            pltpu.VMEM((S + 1, BS, BS), bf16),
            pltpu.SMEM((8, 128), jnp.int32),
            pltpu.SMEM((8, 128), jnp.int32),
            pltpu.VMEM((8, 128), jnp.int32),
            pltpu.VMEM((S + RB + 1, BS, width), f32),
            pltpu.VMEM((PARTS, quarter, BS, width), f32),
            pltpu.VMEM((3, quarter, BS, width), jnp.int16),
            pltpu.VMEM((3, quarter, BS, width), jnp.int16),
            pltpu.VMEM((3, quarter, BS, width), jnp.int16),
            pltpu.VMEM((3, quarter, BS, width), jnp.int16),
            pltpu.VMEM((PARTS * 3, quarter, width), f32),
            pltpu.VMEM((PARTS * 3, quarter, width), f32),
            pltpu.VMEM((PARTS, quarter // 2, BS, width), f32),
            pltpu.VMEM((PARTS, quarter // 2, BS, width), f32),
            pltpu.VMEM((PARTS, quarter // 2, BS, width), f32),
            pltpu.VMEM((R * C, PARTS, width), f32),
            dma(5), dma(4), dma(4),
            dma(PARTS * 2 * R), dma(PARTS * 2 * R), dma(PARTS * 2 * R), dma(PARTS * 2 * R),
            dma(PARTS * 2 * R), dma(PARTS * 2 * R), dma(PARTS * 2 * R), dma(PARTS * 2 * R),
            dma(PARTS * 2), dma(PARTS * 2), dma(PARTS * 2), dma(PARTS * 2),
            dma(PARTS * 3), dma(PARTS * 3), dma(PARTS * 3), dma(PARTS * 3), dma(PARTS), dma(PARTS), dma(R * C), dma(R * C),
        ],
        compiler_params=pltpu.CompilerParams(
            collective_id=0, has_side_effects=True, vmem_limit_bytes=60 << 20
        ),
        cost_estimate=pl.CostEstimate(
            flops=2 * S * BS * BS * PW, bytes_accessed=4 << 20, transcendentals=0
        ),
    )(blocks, table, panel_matrix)
    col_mean = totals.reshape(PW) / (CB * C * BS)
    return squares / (col_mean + epsilon)


def on_device(blocks, owners, places, panel_matrix):
    col_count = lax.axis_size("col")
    row_count = lax.axis_size("row")
    col_blocks = panel_matrix.shape[0]
    block_side = blocks.shape[1]
    panel_width = panel_matrix.shape[2]
    row_blocks = col_blocks * col_count // row_count
    capacity = row_blocks * col_blocks // col_count
    targets = jnp.arange(col_count, dtype=jnp.int32)
    onehot = (owners[:, None] == targets[None, :]).astype(jnp.int32)
    before = jnp.cumsum(onehot, axis=0) - onehot
    bucket_rank = jnp.sum(before * onehot, axis=1)
    slot_index = owners * capacity + bucket_rank
    received = col_count * capacity
    outgoing = (
        jnp.zeros((received, block_side, block_side), blocks.dtype).at[slot_index].set(blocks)
    )
    out_places = jnp.zeros((received,), jnp.int32).at[slot_index].set(places)
    outgoing = outgoing.reshape(col_count, capacity, block_side, block_side)
    out_places = out_places.reshape(col_count, capacity)
    arrived, arrived_places = (
        lax.all_to_all(outgoing, "col", split_axis=0, concat_axis=0, tiled=True),
        lax.all_to_all(out_places, "col", split_axis=0, concat_axis=0, tiled=True),
    )
    arrived = arrived.reshape(received, block_side, block_side)
    arrived_places = arrived_places.reshape(received)
    row_in = arrived_places // col_blocks
    col_in = arrived_places % col_blocks
    panel_full = lax.all_gather(panel_matrix, "row", axis=1, tiled=True)
    group_size = min(32, received)
    turn_count = received // group_size

    def add_group(partial_value, members):
        tile_group, group_rows, group_cols = members
        pieces = panel_full[group_cols]
        product = jnp.einsum("sab,sbp->sap", tile_group, pieces, preferred_element_type=jnp.float32)
        return (partial_value.at[group_rows].add(product), None)

    start_sum = jnp.zeros((row_blocks, block_side, panel_width), jnp.float32)
    partial_value = lax.scan(
        add_group,
        start_sum,
        (
            arrived.reshape(turn_count, group_size, block_side, block_side),
            row_in.reshape(turn_count, group_size),
            col_in.reshape(turn_count, group_size),
        ),
    )[0]
    partial_rows = partial_value.reshape(row_blocks * block_side, panel_width)
    own_rows = lax.psum_scatter(partial_rows, "col", scatter_dimension=0, tiled=True)
    squares = own_rows * own_rows
    totals = lax.psum(jnp.sum(squares, axis=0), ("row", "col"))
    col_mean = totals / (col_blocks * col_count * block_side)
    return squares / (col_mean + epsilon)


def solution(mesh):
    fits = mesh.shape["col"] == 2 * CHIPS and mesh.shape["row"] == 4
    placed = (
        P(("row", "col"), None, None),
        P(("row", "col")),
        P(("row", "col")),
        P("col", "row", None),
    )
    return jax.shard_map(
        fused if fits else on_device, mesh=mesh, in_specs=placed, out_specs=P(("row", "col"), None), check_vma=False
    )
```
